32 devices in a mesh: section: 4 (over x, core), expert: 8 (over z, y).
Axes of the slice: x: 2, y: 2, z: 4, core: 2. Of those that a mesh axis runs over, the one named last changes fastest.
Arguments:
- tokens: bfloat16 [2, 4, 512, 2048], P(None, 'section', 'expert'), may hold values from -24 to 24
- norm_gain: float32 [2048], replicated, may hold values from 0.1 to 1.9
- expert_ids: int32 [2, 4, 512, 2], P(None, 'section', 'expert'), may hold values from 0 to 11, all different within a row; in each aligned block of 64 rows (0 to 63, 64 to 127, ..., all dimensions but the last counted through in order) at most 11 rows name the same one
- route_scores: float32 [2, 4, 512, 2], P(None, 'section', 'expert'), may hold values from 0.1 to 1
- placement: int32 [32], replicated, may hold values from 0 to 11, as said below
- w_gate: bfloat16 [32, 2048, 768], P('expert'), as said below
- w_up: bfloat16 [32, 2048, 768], P('expert'), as said below
- w_down: bfloat16 [32, 768, 2048], P('expert'), as said below
Outputs:
- onward: bfloat16 [2, 4, 512, 2048], P(None, 'section', 'expert')
The draws below stay inside these ranges and needn't reach their ends.
Inputs may be any that keep to these rules, and one draw needn't show every extreme that they name: `expert_ids`: in each micro-batch and section, the 64 rows of one device name each expert at most 11 times, a bound that some block reaches. `placement`: every expert holds two or more slots. `w_gate`: slots with equal placement hold equal gate projections. `w_up`: slots with equal placement hold equal up projections. `w_down`: slots with equal placement hold equal down projections.
All inputs are finite; a program needn't handle non-finite values.
Results may differ from the reference program's by a relative error of at most 0.0039.
Values may be sent and summed in bfloat16 or wider, within the bound.
A program may use at most 128 MiB of HBM per device.

```python
import math
import jax
import jax.numpy as jnp
import numpy as np
from jax import lax

D = 2048
FF = 768
TOP = 2
MB = 2
TOK = 64
SECTIONS = 4
TOKENS = 512
SLOTS = 32
EXPERTS = 12
MOST = 11
N_EXPERT = 8


def slot_experts(key):
    owners = jnp.arange(EXPERTS, dtype=jnp.int32)
    extra = jax.random.randint(jax.random.fold_in(key, 101), (SLOTS - 2 * EXPERTS,), 0, EXPERTS, dtype=jnp.int32)
    table = jnp.concatenate([owners, owners, extra])
    shuffle = jax.random.permutation(jax.random.fold_in(key, 102), SLOTS)
    return table[shuffle].astype(jnp.int32)


def expert_table(key, salt, fan_rows, fan_cols):
    owners = slot_experts(key)
    base = jax.random.normal(jax.random.fold_in(key, salt), (EXPERTS, fan_rows, fan_cols), jnp.float32) * fan_rows ** (-0.5)
    return base[owners].astype(jnp.bfloat16)


def draw_placement(key, part):
    return slot_experts(key)


def draw_w_gate(key, part):
    return expert_table(key, 201, D, FF)


def draw_w_up(key, part):
    return expert_table(key, 202, D, FF)


def draw_w_down(key, part):
    return expert_table(key, 203, FF, D)


def draw_tokens(key, part):
    shape = (MB, SECTIONS, TOKENS, D)
    noise = jnp.clip(jax.random.normal(jax.random.fold_in(key, 302), shape, jnp.float32), -4.0, 4.0)
    columns = jnp.exp(jax.random.uniform(jax.random.fold_in(key, 303), (D,), jnp.float32, math.log(0.3), math.log(3.0)))
    row_scale = jnp.exp(jax.random.uniform(jax.random.fold_in(key, 304), (MB, SECTIONS, TOKENS, 1), jnp.float32, math.log(0.5), math.log(2.0)))
    return (noise * columns * row_scale).astype(jnp.bfloat16)


def block_levels(key, dims, shards, smallest, high):
    loudness = 1.0
    for dim, blocks in shards:
        draws = jax.random.uniform(jax.random.fold_in(jax.random.fold_in(key, 6), dim), (blocks,), jnp.float32, smallest / len(shards), high / len(shards))
        loudness = loudness * jnp.repeat(jnp.exp(draws), dims[dim] // blocks).reshape((-1,) + (1,) * (len(dims) - 1 - dim))
    return loudness


def shared_out(stream_key, own, number, rows, number_of, top, limit, lean):
    ranking = jax.random.permutation(stream_key, number_of)
    packed, ordinary = load_shares(number_of, rows * top, limit, lean, True), load_shares(number_of, rows * top, limit, lean, False)
    places = jnp.arange(number_of)

    def named(lengths, turn):
        used = int((lengths > 0).sum())
        fixed = max(1, used // 4)
        moved = fixed + (places - fixed + turn * (used - fixed)) % max(1, number_of - fixed)
        return jnp.zeros((number_of,), jnp.int32).at[ranking[jnp.where(places < fixed, places, moved)]].set(jnp.asarray(lengths, jnp.int32))

    lengths = jnp.where(number % 4 == 0, named(packed, number // 4), named(ordinary, number - number // 4 - 1))
    mixed = jax.random.permutation(jax.random.fold_in(own, 3), number_of)
    giver, receiver = mixed[0:number_of // 2 * 2:2], mixed[1:number_of // 2 * 2:2]
    room = jnp.minimum(lengths[giver] - 1, limit - lengths[receiver]) // 2
    room = jnp.where((giver == ranking[0]) | (receiver == ranking[0]) | (lengths[receiver] == 0), 0, jnp.maximum(room, 0))
    moved = jax.random.randint(jax.random.fold_in(own, 4), (number_of // 2,), 0, 1 << 20) % (room + 1)
    lengths = lengths.at[giver].add(-moved).at[receiver].add(moved)
    members = jnp.searchsorted(jnp.cumsum(lengths), jnp.arange(rows * top), side="right").astype(jnp.int32)
    listing = members.reshape(top, rows).T
    listing = listing[jax.random.permutation(jax.random.fold_in(own, 1), rows)]
    turn = jax.random.randint(jax.random.fold_in(own, 2), (rows, 1), 0, top)
    return jnp.take_along_axis(listing, (jnp.arange(top)[None, :] + turn) % top, axis=1)


def load_shares(count, total, reach, lean, full):
    loads = [(1 << 20) // math.isqrt(grade ** lean) + 1 for grade in range(1, count + 1)]
    largest = reach if full else min(reach, max(-(-total // count), total * loads[0] // sum(loads)))
    least = 1 if total - largest >= count - 1 else 0
    given, spare = [largest] + [least] * (count - 1), total - largest - least * (count - 1)
    while spare > 0:
        candidates = [i for i in range(1, count) if given[i] < largest] or [i for i in range(1, count) if given[i] < reach]
        pool, remaining = sum([loads[i] for i in candidates]), spare
        for i in candidates:
            more = min(reach - given[i], max(1, remaining * loads[i] // pool), spare)
            given[i] = given[i] + more
            spare = spare - more
    return np.array(given)


def setup_inputs(seed: int = 0) -> dict:
    splits = jax.random.split(jax.random.key(seed), 9)
    tokens = draw_tokens(jax.random.fold_in(splits[8], 71), 0)
    norm_gain = jnp.clip(1.0 + 0.18 * jax.random.normal(splits[1], (D,), jnp.float32), 0.1, 1.9)
    expert_ids_keys = jax.random.split(jax.random.fold_in(splits[2], 1), MB * SECTIONS * TOKENS // TOK)
    expert_ids_turns = jax.random.permutation(jax.random.fold_in(splits[2], 3), MB * SECTIONS * TOKENS // TOK)
    expert_ids = jax.vmap(lambda own, number: shared_out(jax.random.fold_in(splits[2], 2), own, number, TOK, EXPERTS, TOP, MOST, 2))(expert_ids_keys, expert_ids_turns).reshape((MB, SECTIONS, TOKENS, TOP))
    route_scores = jnp.clip(jnp.exp(math.log(1.0) - 2.3025851 * jax.random.uniform(splits[3], (MB, SECTIONS, TOKENS, TOP), jnp.float32) ** block_levels(splits[3], (MB, SECTIONS, TOKENS, TOP), ((1, 4), (2, 8)), -0.2, 0.2)), 0.1, 1.0)
    placement = draw_placement(jax.random.fold_in(splits[8], 71), 0)
    w_gate = draw_w_gate(jax.random.fold_in(splits[8], 71), 0)
    w_up = draw_w_up(jax.random.fold_in(splits[8], 71), 0)
    w_down = draw_w_down(jax.random.fold_in(splits[8], 71), 0)
    return dict(tokens=tokens, norm_gain=norm_gain, expert_ids=expert_ids, route_scores=route_scores, placement=placement, w_gate=w_gate, w_up=w_up, w_down=w_down)


EPSILON = 1e-06

def reference(tokens, norm_gain, expert_ids, route_scores, placement, w_gate, w_up, w_down):
    expert_range = jnp.arange(EXPERTS, dtype=jnp.int32)
    slot_range = jnp.arange(SLOTS, dtype=jnp.int32)
    first_slot = lax.optimization_barrier(jnp.min(jnp.where(placement[None, :] == expert_range[:, None], slot_range[None, :], SLOTS), axis=1)).astype(jnp.int32)
    capacity = N_EXPERT * MOST
    routed = TOKENS * TOP
    lane = jnp.arange(capacity, dtype=jnp.int32)

    def one_block(block):
        rows, chosen, scores = block
        values = rows.astype(jnp.float32)
        scale = lax.rsqrt(lax.optimization_barrier(jnp.mean(values * values, axis=-1, keepdims=True)) + EPSILON)
        normed = (values * scale * norm_gain.astype(jnp.float32)).astype(jnp.bfloat16)
        probs = scores / lax.optimization_barrier(jnp.sum(scores, axis=1, keepdims=True))
        flat_ids = chosen.reshape(-1).astype(jnp.int32)
        order = jnp.argsort(flat_ids, stable=True).astype(jnp.int32)
        counts = lax.optimization_barrier(jnp.sum((flat_ids[:, None] == expert_range[None, :]).astype(jnp.int32), axis=0))
        starts = (jnp.cumsum(counts) - counts).astype(jnp.int32)

        def one_expert(expert):
            lookup = jnp.clip(starts[expert] + lane, 0, routed - 1).astype(jnp.int32)
            index = order[lookup]
            valid = lane < counts[expert]
            inputs = normed[index // TOP]
            slot = first_slot[expert]
            gate = jnp.dot(inputs, w_gate[slot], preferred_element_type=jnp.float32)
            up = jnp.dot(inputs, w_up[slot], preferred_element_type=jnp.float32)
            hidden = (jax.nn.silu(gate) * up).astype(jnp.bfloat16)
            output = jnp.dot(hidden, w_down[slot], preferred_element_type=jnp.float32).astype(jnp.bfloat16)
            kept = jnp.where(valid[:, None], output.astype(jnp.float32), jnp.zeros_like(output, dtype=jnp.float32))
            return (kept, index)
        outputs, indices = lax.map(one_expert, expert_range)
        placed = jnp.zeros((routed, D), jnp.float32).at[indices.reshape(-1)].add(outputs.reshape(-1, D))
        moe = lax.optimization_barrier(jnp.sum(probs[:, :, None] * placed.reshape(TOKENS, TOP, D), axis=1))
        return (values + moe).astype(jnp.bfloat16)
    blocks = lax.map(one_block, (tokens.reshape(MB * SECTIONS, TOKENS, D), expert_ids.reshape(MB * SECTIONS, TOKENS, TOP), route_scores.reshape(MB * SECTIONS, TOKENS, TOP)))
    mixed = blocks.reshape(MB, SECTIONS, TOKENS, D)
    empty = jnp.zeros((1, TOKENS, D), mixed.dtype)
    forward = jnp.concatenate([empty, mixed[0, :-1]], axis=0)
    backward = jnp.concatenate([mixed[1, 1:], empty], axis=0)
    return jnp.stack([forward, backward], axis=0)
```

```python
import functools

import jax
import jax.numpy as jnp
from jax import lax
from jax.experimental import pallas as pl
from jax.experimental.pallas import tpu as pltpu
from jax.sharding import PartitionSpec as P

EPSILON = 1e-06
STRIDE = 1024
MARK = 1 << 20
MESH = pl.DeviceIdType.MESH
COLUMNS = 256


def round_up(value, to):
    return (value + to - 1) // to * to


def split_columns(width):
    return COLUMNS if width % COLUMNS == 0 else width


def layer(
    near, far, slots,
    tokens, gain, ids, scores, code_near, code_far, slot_near, slot_far, w_gate, w_up, w_down,
    out,
    gate_buf, up_buf, down_buf, normed, hits_near, hits_far, hidden, mixed,
    send_n, send_f, recv_n, recv_f, done_n, done_f, back_n, back_f,
    weight_sem, to_n, from_n, to_f, from_f, ret_to_n, ret_from_n, ret_to_f, ret_from_f, relay_to, relay_from,
):
    section = lax.axis_index("section")
    sections = lax.axis_size("section")
    me = lax.axis_index("expert")
    peers = lax.axis_size("expert")
    half = peers // 2
    mine = me % half
    side = me // half
    micros, rows, width = tokens.shape
    top = ids.shape[2]
    experts = STRIDE

    loads = []
    for slot in range(slots):
        for kind, (src, dst) in enumerate(((w_gate, gate_buf), (w_up, up_buf), (w_down, down_buf))):
            copy = pltpu.make_async_copy(src.at[slot], dst.at[slot], weight_sem.at[kind, slot])
            copy.start()
            loads.append(copy)

    barrier = pltpu.get_barrier_semaphore()

    def greet(step, carry):
        pl.semaphore_signal(
            barrier, inc=1, device_id=(section, (me + step) % peers), device_id_type=MESH
        )
        return carry

    lax.fori_loop(1, peers, greet, 0)

    @pl.when(section > 0)
    def _():
        pl.semaphore_signal(barrier, inc=1, device_id=(section - 1, me), device_id_type=MESH)

    @pl.when(section < sections - 1)
    def _():
        pl.semaphore_signal(barrier, inc=1, device_id=(section + 1, me), device_id_type=MESH)

    lane = lax.broadcasted_iota(jnp.int32, (rows, 128), 1)
    lower = (
        lax.broadcasted_iota(jnp.int32, (rows, rows), 0)
        > lax.broadcasted_iota(jnp.int32, (rows, rows), 1)
    ).astype(jnp.bfloat16)
    mixing = []
    for micro in range(micros):
        values = tokens[micro].astype(jnp.float32)
        scale = lax.rsqrt(jnp.mean(values * values, axis=-1, keepdims=True) + EPSILON)
        normed[micro] = (values * scale * gain[...]).astype(jnp.bfloat16)
        ones = [(ids[micro][:, k : k + 1] == lane).astype(jnp.float32) for k in range(top)]
        both = functools.reduce(jnp.add, ones)
        before = jnp.dot(lower, both.astype(jnp.bfloat16), preferred_element_type=jnp.float32)
        chosen = scores[micro]
        probs = chosen / jnp.sum(chosen, axis=1, keepdims=True)
        take_n = take_f = mix_n = mix_f = 0.0
        for k in range(top):
            rank = jnp.sum(before * ones[k], axis=1, keepdims=True).astype(jnp.int32)
            code = ids[micro][:, k : k + 1] * STRIDE + rank
            in_n = (code == code_near[...]).astype(jnp.float32)
            in_f = (code + micro * MARK == code_far[...]).astype(jnp.float32)
            take_n = take_n + in_n
            take_f = take_f + in_f
            mix_n = mix_n + in_n * probs[:, k : k + 1]
            mix_f = mix_f + in_f * probs[:, k : k + 1]
        hits_near[micro] = take_n.astype(jnp.bfloat16)
        hits_far[micro] = take_f.astype(jnp.bfloat16)
        mixing.append((mix_n, mix_f))

    def gather(hits, source):
        return lax.dot_general(
            hits, source, (((0,), (0,)), ((), ())), preferred_element_type=jnp.float32
        )

    send_f[...] = (
        sum(gather(hits_far[micro], normed[micro]) for micro in range(micros))
        .astype(jnp.bfloat16)
        .reshape(send_f.shape)
    )

    greeted = (
        peers - 1 + (section > 0).astype(jnp.int32) + (section < sections - 1).astype(jnp.int32)
    )
    pl.semaphore_wait(barrier, greeted)

    def far_copy(step, src, dst, sent, arrived):
        there = (mine + step) % half
        return pltpu.make_async_remote_copy(
            src_ref=src.at[there],
            dst_ref=dst.at[mine],
            send_sem=sent.at[step],
            recv_sem=arrived.at[step],
            device_id=(section, (1 - side) * half + there),
            device_id_type=MESH,
        )

    def near_copy(micro, step, src, dst, sent, arrived):
        there = (mine + step) % half
        return pltpu.make_async_remote_copy(
            src_ref=src.at[micro, there],
            dst_ref=dst.at[micro, mine],
            send_sem=sent.at[micro, step],
            recv_sem=arrived.at[micro, step],
            device_id=(section, side * half + there),
            device_id_type=MESH,
        )

    def each(first, act):
        def step_body(step, carry):
            act(step)
            return carry

        lax.fori_loop(first, half, step_body, 0)

    each(0, lambda step: far_copy(step, send_f, recv_f, to_f, from_f).start())
    for micro in range(micros):
        send_n[micro] = (
            gather(hits_near[micro], normed[micro]).astype(jnp.bfloat16).reshape(send_n.shape[1:])
        )
        each(1, lambda step: near_copy(micro, step, send_n, recv_n, to_n, from_n).start())
        recv_n[micro, mine] = send_n[micro, mine]

    def experts_of(count, inputs, owner, store):
        ff = gate_buf.shape[2]
        block = split_columns(ff)
        per = ff // block

        def up_body(step, carry):
            slot = step // per
            cols = pl.ds(pl.multiple_of((step % per) * block, block), block)
            x = inputs()
            gate = jnp.dot(x, gate_buf[slot, :, cols], preferred_element_type=jnp.float32)
            up = jnp.dot(x, up_buf[slot, :, cols], preferred_element_type=jnp.float32)
            unit = gate / (1.0 + jnp.exp(-gate)) * up
            unit = jnp.where(owner == slot, unit, 0.0)
            hidden[step, :count] = unit.astype(jnp.bfloat16)
            return carry

        lax.fori_loop(0, slots * per, up_body, 0)
        wide = split_columns(width)

        def down_body(step, carry):
            cols = pl.ds(pl.multiple_of(step * wide, wide), wide)
            total = jnp.zeros((count, wide), jnp.float32)
            for slot in range(slots):
                for part in range(per):
                    total = total + jnp.dot(
                        hidden[slot * per + part, :count],
                        down_buf[slot, part * block : (part + 1) * block, cols],
                        preferred_element_type=jnp.float32,
                    )
            store(cols, total.astype(jnp.bfloat16))
            return carry

        lax.fori_loop(0, width // wide, down_body, 0)

    rows_n, rows_f = half * near, half * far * micros

    each(0, lambda step: far_copy(step, send_f, recv_f, to_f, from_f).wait_recv())
    each(1, lambda step: near_copy(0, step, send_n, recv_n, to_n, from_n).wait_recv())
    for copy in loads:
        copy.wait()

    def store_first(cols, value):
        done_f[:, :, cols] = value[:rows_f].reshape(half, far * micros, value.shape[1])
        done_n[0, :, :, cols] = value[rows_f:].reshape(half, near, value.shape[1])

    experts_of(
        rows_f + rows_n,
        lambda: jnp.concatenate(
            [recv_f[...].reshape(rows_f, width), recv_n[0].reshape(rows_n, width)], axis=0
        ),
        jnp.concatenate([slot_far[...], slot_near[...]], axis=0),
        store_first,
    )
    each(0, lambda step: far_copy(step, done_f, back_f, ret_to_f, ret_from_f).start())
    each(1, lambda step: near_copy(0, step, done_n, back_n, ret_to_n, ret_from_n).start())
    back_n[0, mine] = done_n[0, mine]

    for micro in range(1, micros):
        each(1, lambda step: near_copy(micro, step, send_n, recv_n, to_n, from_n).wait_recv())

        def store_next(cols, value):
            done_n[micro, :, :, cols] = value.reshape(half, near, value.shape[1])

        experts_of(
            rows_n, lambda: recv_n[micro].reshape(rows_n, width), slot_near[...], store_next
        )
        each(1, lambda step: near_copy(micro, step, done_n, back_n, ret_to_n, ret_from_n).start())
        back_n[micro, mine] = done_n[micro, mine]

    def weighed(mix, values):
        high = mix.astype(jnp.bfloat16)
        low = (mix - high.astype(jnp.float32)).astype(jnp.bfloat16)
        return jnp.dot(high, values, preferred_element_type=jnp.float32) + jnp.dot(
            low, values, preferred_element_type=jnp.float32
        )

    def relay(micro, by):
        return pltpu.make_async_remote_copy(
            src_ref=mixed.at[micro],
            dst_ref=out.at[micro],
            send_sem=relay_to.at[micro],
            recv_sem=relay_from.at[micro],
            device_id=(section + by, me),
            device_id_type=MESH,
        )

    each(0, lambda step: far_copy(step, done_f, back_f, ret_to_f, ret_from_f).wait_recv())
    sends = ((0, 1, section < sections - 1, section > 0), (1, -1, section > 0, section < sections - 1))
    for micro, by, gives, gets in sends:
        each(1, lambda step: near_copy(micro, step, done_n, back_n, ret_to_n, ret_from_n).wait_recv())
        mix_n, mix_f = mixing[micro]
        total = tokens[micro].astype(jnp.float32)
        total = total + weighed(mix_f, back_f[...].reshape(rows_f, width))
        total = total + weighed(mix_n, back_n[micro].reshape(rows_n, width))
        mixed[micro] = total.astype(jnp.bfloat16)

        @pl.when(gives)
        def _():
            relay(micro, by).start()

        @pl.when(jnp.logical_not(gets))
        def _():
            out[micro] = jnp.zeros(out.shape[1:], out.dtype)

    each(0, lambda step: far_copy(step, send_f, recv_f, to_f, from_f).wait_send())
    each(0, lambda step: far_copy(step, done_f, back_f, ret_to_f, ret_from_f).wait_send())
    for micro in range(micros):
        each(1, lambda step: near_copy(micro, step, send_n, recv_n, to_n, from_n).wait_send())
        each(1, lambda step: near_copy(micro, step, done_n, back_n, ret_to_n, ret_from_n).wait_send())
    for micro, by, gives, gets in sends:

        @pl.when(gives)
        def _():
            relay(micro, by).wait_send()

        @pl.when(gets)
        def _():
            relay(micro, by).wait_recv()


def places(placement, devices, slot_cap, near, far):
    slots = placement.shape[0]
    slot_range = jnp.arange(slots, dtype=jnp.int32)
    same = placement[:, None] == placement[None, :]
    copies = jnp.sum(same, axis=1, dtype=jnp.int32)
    replica = jnp.sum(same & (slot_range[None, :] < slot_range[:, None]), axis=1, dtype=jnp.int32)
    index = jnp.arange(slot_cap, dtype=jnp.int32)
    code = placement[:, None] * STRIDE + index[None, :] * copies[:, None] + replica[:, None]
    per = slots // devices
    code = code.reshape(devices, per * slot_cap)
    owner = jnp.broadcast_to(jnp.arange(per, dtype=jnp.int32)[:, None], (per, slot_cap)).reshape(-1)
    fill_n, fill_f = near - per * slot_cap, far - per * slot_cap
    code_n = jnp.pad(code, ((0, 0), (0, fill_n)), constant_values=-1)
    code_f = jnp.pad(code, ((0, 0), (0, fill_f)), constant_values=-1)
    return code_n, code_f, jnp.pad(owner, (0, fill_n)), jnp.pad(owner, (0, fill_f))


def body(tokens, norm_gain, expert_ids, route_scores, placement, w_gate, w_up, w_down):
    devices = lax.axis_size("expert")
    half = devices // 2
    side = lax.axis_index("expert") // half
    slots = w_gate.shape[0]
    ff = w_gate.shape[2]
    micros, _, rows, width = tokens.shape
    top = expert_ids.shape[3]
    experts = placement.shape[0] * 3 // 8
    most = (rows * top + experts - 1) // experts
    slot_cap = (most + 1) // 2
    near = round_up(slots * slot_cap, 16)
    far = round_up(slots * slot_cap, 8)
    code_n, code_f, owner_n, owner_f = places(placement, devices, slot_cap, near, far)

    code_near = lax.dynamic_slice_in_dim(code_n, side * half, half, 0).reshape(1, half * near)
    code_there = lax.dynamic_slice_in_dim(code_f, (1 - side) * half, half, 0)
    marks = jnp.arange(micros, dtype=jnp.int32) * MARK
    code_far = jnp.where(
        code_there[:, None, :] >= 0, code_there[:, None, :] + marks[None, :, None], -1
    ).reshape(1, half * micros * far)
    slot_near = jnp.broadcast_to(owner_n[None, :], (half, near)).reshape(half * near, 1)
    slot_far = jnp.broadcast_to(owner_f[None, None, :], (half, micros, far)).reshape(-1, 1)

    rows_n, rows_f = half * near, half * micros * far
    vmem = pl.BlockSpec(memory_space=pltpu.VMEM)
    block = split_columns(ff)
    n_shape = (micros, half, near, width)
    f_shape = (half, micros * far, width)
    bf16 = jnp.bfloat16
    dma = pltpu.SemaphoreType.DMA
    result = pl.pallas_call(
        functools.partial(layer, near, far, slots),
        out_shape=jax.ShapeDtypeStruct((micros, rows, width), bf16),
        in_specs=[vmem] * 8 + [pl.BlockSpec(memory_space=pl.ANY)] * 3,
        out_specs=vmem,
        scratch_shapes=[
            pltpu.VMEM(w_gate.shape, bf16),
            pltpu.VMEM(w_up.shape, bf16),
            pltpu.VMEM(w_down.shape, bf16),
            pltpu.VMEM((micros, rows, width), bf16),
            pltpu.VMEM((micros, rows, rows_n), bf16),
            pltpu.VMEM((micros, rows, rows_f), bf16),
            pltpu.VMEM((slots * (ff // block), rows_n + rows_f, block), bf16),
            pltpu.VMEM((micros, rows, width), bf16),
            pltpu.VMEM(n_shape, bf16),
            pltpu.VMEM(f_shape, bf16),
            pltpu.VMEM(n_shape, bf16),
            pltpu.VMEM(f_shape, bf16),
            pltpu.VMEM(n_shape, bf16),
            pltpu.VMEM(f_shape, bf16),
            pltpu.VMEM(n_shape, bf16),
            pltpu.VMEM(f_shape, bf16),
            dma((3, slots)),
            dma((micros, half)),
            dma((micros, half)),
            dma((half,)),
            dma((half,)),
            dma((micros, half)),
            dma((micros, half)),
            dma((half,)),
            dma((half,)),
            dma((micros,)),
            dma((micros,)),
        ],
        compiler_params=pltpu.CompilerParams(
            collective_id=0, has_side_effects=True, vmem_limit_bytes=62 << 20
        ),
    )(
        tokens[:, 0], norm_gain[None, :], expert_ids[:, 0], route_scores[:, 0],
        code_near, code_far, slot_near, slot_far, w_gate, w_up, w_down,
    )
    return result[:, None]


def solution(mesh):
    in_specs = (
        P(None, "section", "expert", None),
        P(),
        P(None, "section", "expert", None),
        P(None, "section", "expert", None),
        P(),
        P("expert", None, None),
        P("expert", None, None),
        P("expert", None, None),
    )
    out_specs = P(None, "section", "expert", None)
    return jax.shard_map(body, mesh=mesh, in_specs=in_specs, out_specs=out_specs, check_vma=False)
```

```python
import functools
import math

import jax
import jax.numpy as jnp
from jax import lax
from jax.experimental import pallas as pl
from jax.experimental.pallas import tpu as pltpu
from jax.sharding import PartitionSpec as P

EPSILON = 1e-06
STRIDE = 1024
MARK = 1 << 20
MESH = pl.DeviceIdType.MESH
COLUMNS = 256


def round_up(value, to):
    return (value + to - 1) // to * to


def split_columns(width):
    return COLUMNS if width % COLUMNS == 0 else width


def layer(
    near, far, slots, experts,
    tokens, gain, ids, scores, table, w_gate, w_up, w_down,
    out,
    gate_buf, up_buf, down_buf, normed, hits_near, hits_far, hidden, mixed,
    send_n, send_f, recv_n, recv_f, done_n, done_f, back_n, back_f,
    weight_sem, to_n, from_n, to_f, from_f, ret_to_n, ret_from_n, ret_to_f, ret_from_f, relay_to, relay_from,
):
    section = lax.axis_index("section")
    sections = lax.axis_size("section")
    me = lax.axis_index("expert")
    peers = lax.axis_size("expert")
    half = peers // 2
    mine = me % half
    side = me // half
    micros, rows, width = tokens.shape
    top = ids.shape[1]
    rows_n, rows_f = half * near, half * far * micros

    loads = []
    for slot in range(slots):
        for kind, (src, dst) in enumerate(((w_gate, gate_buf), (w_up, up_buf), (w_down, down_buf))):
            copy = pltpu.make_async_copy(src.at[slot], dst.at[slot], weight_sem.at[kind, slot])
            copy.start()
            loads.append(copy)

    barrier = pltpu.get_barrier_semaphore()

    def greet(step, carry):
        pl.semaphore_signal(
            barrier, inc=1, device_id=(section, (me + step) % peers), device_id_type=MESH
        )
        return carry

    lax.fori_loop(1, peers, greet, 0)

    @pl.when(section > 0)
    def _():
        pl.semaphore_signal(barrier, inc=1, device_id=(section - 1, me), device_id_type=MESH)

    @pl.when(section < sections - 1)
    def _():
        pl.semaphore_signal(barrier, inc=1, device_id=(section + 1, me), device_id_type=MESH)

    kinds = round_up(experts, 16)
    kind = lax.broadcasted_iota(jnp.int32, (kinds, rows), 0)
    earlier = (
        lax.broadcasted_iota(jnp.int32, (rows, rows), 0)
        < lax.broadcasted_iota(jnp.int32, (rows, rows), 1)
    ).astype(jnp.bfloat16)
    code_near, code_far = table[:rows_n, 0:1], table[rows_n:, 0:1]
    mixing = []
    for micro in range(micros):
        values = tokens[micro].astype(jnp.float32)
        scale = lax.rsqrt(jnp.mean(values * values, axis=-1, keepdims=True) + EPSILON)
        normed[micro] = (values * scale * gain[...]).astype(jnp.bfloat16)
        ones = [(ids[micro, k : k + 1, :] == kind).astype(jnp.float32) for k in range(top)]
        both = functools.reduce(jnp.add, ones)
        before = jnp.dot(both.astype(jnp.bfloat16), earlier, preferred_element_type=jnp.float32)
        chosen = [scores[micro, k : k + 1, :] for k in range(top)]
        whole = functools.reduce(jnp.add, chosen)
        take_n = take_f = mix_n = mix_f = 0.0
        for k in range(top):
            rank = jnp.sum(before * ones[k], axis=0, keepdims=True).astype(jnp.int32)
            code = ids[micro, k : k + 1, :] * STRIDE + rank
            prob = chosen[k] / whole
            in_n = (code == code_near).astype(jnp.float32)
            in_f = (code + micro * MARK == code_far).astype(jnp.float32)
            take_n = take_n + in_n
            take_f = take_f + in_f
            mix_n = mix_n + in_n * prob
            mix_f = mix_f + in_f * prob
        hits_near[micro] = take_n.astype(jnp.bfloat16)
        hits_far[micro] = take_f.astype(jnp.bfloat16)
        mixing.append((mix_n, mix_f))

    def gather(hits, source):
        return jnp.dot(hits, source, preferred_element_type=jnp.float32)

    send_f[...] = (
        sum(gather(hits_far[micro], normed[micro]) for micro in range(micros))
        .astype(jnp.bfloat16)
        .reshape(send_f.shape)
    )

    greeted = (
        peers - 1 + (section > 0).astype(jnp.int32) + (section < sections - 1).astype(jnp.int32)
    )
    pl.semaphore_wait(barrier, greeted)

    def far_copy(step, src, dst, sent, arrived):
        there = (mine + step) % half
        return pltpu.make_async_remote_copy(
            src_ref=src.at[there],
            dst_ref=dst.at[mine],
            send_sem=sent.at[step],
            recv_sem=arrived.at[step],
            device_id=(section, (1 - side) * half + there),
            device_id_type=MESH,
        )

    def near_copy(micro, step, src, dst, sent, arrived):
        there = (mine + step) % half
        return pltpu.make_async_remote_copy(
            src_ref=src.at[micro, there],
            dst_ref=dst.at[micro, mine],
            send_sem=sent.at[micro, step],
            recv_sem=arrived.at[micro, step],
            device_id=(section, side * half + there),
            device_id_type=MESH,
        )

    def each(first, act):
        def step_body(step, carry):
            act(step)
            return carry

        lax.fori_loop(first, half, step_body, 0)

    each(0, lambda step: far_copy(step, send_f, recv_f, to_f, from_f).start())
    for micro in range(micros):
        send_n[micro] = (
            gather(hits_near[micro], normed[micro]).astype(jnp.bfloat16).reshape(send_n.shape[1:])
        )
        each(1, lambda step: near_copy(micro, step, send_n, recv_n, to_n, from_n).start())
        recv_n[micro, mine] = send_n[micro, mine]

    def experts_of(count, inputs, owner, store):
        ff = gate_buf.shape[2]
        block = split_columns(ff)
        per = ff // block

        def up_body(step, carry):
            slot = step // per
            cols = pl.ds(pl.multiple_of((step % per) * block, block), block)
            x = inputs()
            gate = jnp.dot(x, gate_buf[slot, :, cols], preferred_element_type=jnp.float32)
            up = jnp.dot(x, up_buf[slot, :, cols], preferred_element_type=jnp.float32)
            unit = gate / (1.0 + jnp.exp(-gate)) * up
            unit = jnp.where(owner == slot, unit, 0.0)
            hidden[step, :count] = unit.astype(jnp.bfloat16)
            return carry

        lax.fori_loop(0, slots * per, up_body, 0)
        wide = split_columns(width)

        def down_body(step, carry):
            cols = pl.ds(pl.multiple_of(step * wide, wide), wide)
            total = jnp.zeros((count, wide), jnp.float32)
            for slot in range(slots):
                for part in range(per):
                    total = total + jnp.dot(
                        hidden[slot * per + part, :count],
                        down_buf[slot, part * block : (part + 1) * block, cols],
                        preferred_element_type=jnp.float32,
                    )
            store(cols, total.astype(jnp.bfloat16))
            return carry

        lax.fori_loop(0, width // wide, down_body, 0)

    each(0, lambda step: far_copy(step, send_f, recv_f, to_f, from_f).wait_recv())
    each(1, lambda step: near_copy(0, step, send_n, recv_n, to_n, from_n).wait_recv())
    for copy in loads:
        copy.wait()

    def store_first(cols, value):
        done_f[:, :, cols] = value[:rows_f].reshape(half, far * micros, value.shape[1])
        done_n[0, :, :, cols] = value[rows_f:].reshape(half, near, value.shape[1])

    experts_of(
        rows_f + rows_n,
        lambda: jnp.concatenate(
            [recv_f[...].reshape(rows_f, width), recv_n[0].reshape(rows_n, width)], axis=0
        ),
        jnp.concatenate([table[rows_n:, 1:2], table[:rows_n, 1:2]], axis=0),
        store_first,
    )
    each(0, lambda step: far_copy(step, done_f, back_f, ret_to_f, ret_from_f).start())
    each(1, lambda step: near_copy(0, step, done_n, back_n, ret_to_n, ret_from_n).start())
    back_n[0, mine] = done_n[0, mine]

    for micro in range(1, micros):
        each(1, lambda step: near_copy(micro, step, send_n, recv_n, to_n, from_n).wait_recv())

        def store_next(cols, value):
            done_n[micro, :, :, cols] = value.reshape(half, near, value.shape[1])

        experts_of(
            rows_n, lambda: recv_n[micro].reshape(rows_n, width), table[:rows_n, 1:2], store_next
        )
        each(1, lambda step: near_copy(micro, step, done_n, back_n, ret_to_n, ret_from_n).start())
        back_n[micro, mine] = done_n[micro, mine]

    def weighed(mix, values):
        high = mix.astype(jnp.bfloat16)
        low = (mix - high.astype(jnp.float32)).astype(jnp.bfloat16)
        rule = (((0,), (0,)), ((), ()))
        return lax.dot_general(
            high, values, rule, preferred_element_type=jnp.float32
        ) + lax.dot_general(low, values, rule, preferred_element_type=jnp.float32)

    def relay(micro, by):
        return pltpu.make_async_remote_copy(
            src_ref=mixed.at[micro],
            dst_ref=out.at[micro],
            send_sem=relay_to.at[micro],
            recv_sem=relay_from.at[micro],
            device_id=(section + by, me),
            device_id_type=MESH,
        )

    each(0, lambda step: far_copy(step, done_f, back_f, ret_to_f, ret_from_f).wait_recv())
    sends = ((0, 1, section < sections - 1, section > 0), (1, -1, section > 0, section < sections - 1))
    for micro, by, gives, gets in sends:
        each(1, lambda step: near_copy(micro, step, done_n, back_n, ret_to_n, ret_from_n).wait_recv())
        mix_n, mix_f = mixing[micro]
        total = tokens[micro].astype(jnp.float32)
        total = total + weighed(mix_f, back_f[...].reshape(rows_f, width))
        total = total + weighed(mix_n, back_n[micro].reshape(rows_n, width))
        mixed[micro] = total.astype(jnp.bfloat16)

        @pl.when(gives)
        def _():
            relay(micro, by).start()

        @pl.when(jnp.logical_not(gets))
        def _():
            out[micro] = jnp.zeros(out.shape[1:], out.dtype)

    each(0, lambda step: far_copy(step, send_f, recv_f, to_f, from_f).wait_send())
    each(0, lambda step: far_copy(step, done_f, back_f, ret_to_f, ret_from_f).wait_send())
    for micro in range(micros):
        each(1, lambda step: near_copy(micro, step, send_n, recv_n, to_n, from_n).wait_send())
        each(1, lambda step: near_copy(micro, step, done_n, back_n, ret_to_n, ret_from_n).wait_send())
    for micro, by, gives, gets in sends:

        @pl.when(gives)
        def _():
            relay(micro, by).wait_send()

        @pl.when(gets)
        def _():
            relay(micro, by).wait_recv()


def plain_table(placement, devices, slot_cap, near, far, micros):
    half = devices // 2
    side = lax.axis_index("expert") // half
    slots = placement.shape[0]
    per = slots // devices
    slot_range = jnp.arange(slots, dtype=jnp.int32)
    same = placement[:, None] == placement[None, :]
    copies = jnp.sum(same, axis=1, dtype=jnp.int32)
    replica = jnp.sum(same & (slot_range[None, :] < slot_range[:, None]), axis=1, dtype=jnp.int32)
    index = jnp.arange(slot_cap, dtype=jnp.int32)
    code = placement[:, None] * STRIDE + index[None, :] * copies[:, None] + replica[:, None]
    code = code.reshape(devices, per * slot_cap)
    owner = jnp.broadcast_to(jnp.arange(per, dtype=jnp.int32)[:, None], (per, slot_cap)).reshape(-1)
    fill_n, fill_f = near - per * slot_cap, far - per * slot_cap
    code_n = jnp.pad(code, ((0, 0), (0, fill_n)), constant_values=-1)
    code_f = jnp.pad(code, ((0, 0), (0, fill_f)), constant_values=-1)
    code_n = lax.dynamic_slice_in_dim(code_n, side * half, half, 0).reshape(-1)
    code_f = lax.dynamic_slice_in_dim(code_f, (1 - side) * half, half, 0)[:, None, :]
    marks = jnp.arange(micros, dtype=jnp.int32)[None, :, None] * MARK
    code_f = jnp.where(code_f >= 0, code_f + marks, -1).reshape(-1)
    slot_n = jnp.tile(jnp.pad(owner, (0, fill_n)), half)
    slot_f = jnp.tile(jnp.pad(owner, (0, fill_f)), half * micros)
    columns = jnp.stack(
        [jnp.concatenate([code_n, code_f]), jnp.concatenate([slot_n, slot_f])], axis=1
    )
    return jnp.pad(columns, ((0, 0), (0, 126)))


def plan(near, far, micros, experts, most, held, table, fits):
    devices, per = held.shape
    half = devices // 2
    me = lax.axis_index("expert")
    side = me // half
    f32 = jnp.float32
    shape = (devices, 128)
    lane = lax.broadcasted_iota(jnp.int32, shape, 1)
    device = lax.broadcasted_iota(jnp.int32, shape, 0)
    from_half = lane // 64
    attempt = lane % 64
    strides = [a for a in range(1, experts) if math.gcd(a, experts) == 1][: max(1, 64 // experts)]
    turn = attempt // experts
    stride = jnp.full(shape, strides[0], jnp.int32)
    for i, a in enumerate(strides):
        stride = jnp.where(turn == i, a, stride)
    weight = jnp.where(device // half == from_half, far, near)
    limit = near * far
    owned = [held[:, j : j + 1] for j in range(per)]
    order, holds = [], []
    now = attempt % experts
    for _ in range(experts):
        order.append(now)
        holds.append(functools.reduce(jnp.logical_or, [o == now for o in owned]))
        now = now + stride
        now = jnp.where(now >= experts, now - experts, now)
    load = jnp.zeros(shape, jnp.int32)
    given = [jnp.zeros(shape, jnp.int32)] * experts
    chunks = [most - most // 2, most // 2]
    for _ in range(2):
        for step in range(experts):
            load = load - given[step]
            share = jnp.zeros(shape, jnp.int32)
            for chunk in chunks:
                key = jnp.where(holds[step], (load + chunk) * weight * devices + device, 1 << 30)
                best = jnp.min(key, axis=0, keepdims=True)
                more = jnp.where(key == best, chunk, 0)
                load = load + more
                share = share + more
            given[step] = share
    worst = jnp.max(load * weight, axis=0, keepdims=True)
    lane_row = lax.broadcasted_iota(jnp.int32, (1, 128), 1)
    rating = worst * 128 + lane_row
    half_row = lane_row // 64
    ratings = [
        jnp.min(jnp.where(half_row == h, rating, 1 << 30), axis=1, keepdims=True) for h in range(2)
    ]
    fits[...] = jnp.broadcast_to(
        (jnp.maximum(ratings[0], ratings[1]) < (limit + 1) * 128).astype(jnp.int32), fits.shape
    )

    def columns(from_side, length, width, period, to_device):
        rating_there = jnp.where(from_side == 0, ratings[0], ratings[1])
        picked = (rating == rating_there) & (half_row == from_side)
        amount = jnp.zeros(shape, f32)
        kinds = jnp.zeros((1, 128), f32)
        for step in range(experts):
            mine = jnp.sum(jnp.where(picked, given[step], 0).astype(f32), axis=1, keepdims=True)
            kind = jnp.sum(
                jnp.where(picked, order[step][:1], 0).astype(f32), axis=1, keepdims=True
            )
            amount = amount + jnp.where(lane == step, mine, 0.0)
            kinds = kinds + jnp.where(lane_row == step, kind, 0.0)
        first = jnp.dot(
            (
                lax.broadcasted_iota(jnp.int32, (devices, devices), 1)
                < lax.broadcasted_iota(jnp.int32, (devices, devices), 0)
            ).astype(f32),
            amount,
            preferred_element_type=f32,
        )
        ahead = jnp.dot(
            amount,
            (
                lax.broadcasted_iota(jnp.int32, (128, 128), 0)
                < lax.broadcasted_iota(jnp.int32, (128, 128), 1)
            ).astype(f32),
            preferred_element_type=f32,
        )
        local = jnp.zeros(shape, f32)
        for j in reversed(range(per)):
            local = jnp.where(owned[j].astype(f32) == kinds, float(j), local)
        row = lax.broadcasted_iota(jnp.int32, (length, 1), 0)
        place = (row % period).astype(f32)
        target = (
            lax.broadcasted_iota(jnp.int32, (length, devices), 1) == to_device(row // width)
        ).astype(f32)

        def spread(values):
            return jnp.dot(target, values, preferred_element_type=f32)

        start = spread(ahead)
        inside = ((place >= start) & (place < start + spread(amount))).astype(f32)
        numbers = kinds * STRIDE + place - start + spread(first)
        code = jnp.sum(inside * (numbers + 1.0), axis=1, keepdims=True).astype(jnp.int32) - 1
        slot = jnp.sum(inside * spread(local), axis=1, keepdims=True).astype(jnp.int32)
        return code, slot, row

    rows_n, rows_f = half * near, half * far * micros
    code_n, _, _ = columns(side, rows_n, near, near, lambda block: side * half + block)
    code_f, _, row_f = columns(
        side, rows_f, far * micros, far, lambda block: (1 - side) * half + block
    )
    code_f = jnp.where(code_f >= 0, code_f + row_f % (far * micros) // far * MARK, -1)
    _, slot_n, _ = columns(side, rows_n, near, near, lambda block: me + 0 * block)
    _, slot_f, _ = columns(1 - side, rows_f, far * micros, far, lambda block: me + 0 * block)
    column = lax.broadcasted_iota(jnp.int32, (rows_n, 128), 1)
    table[:rows_n] = jnp.where(column == 0, code_n, slot_n)
    column = lax.broadcasted_iota(jnp.int32, (rows_f, 128), 1)
    table[rows_n:] = jnp.where(column == 0, code_f, slot_f)


def routed(call, near, far, experts, table, tokens, gain, ids, scores, w_gate, w_up, w_down):
    devices = lax.axis_size("expert")
    half = devices // 2
    slots = w_gate.shape[0]
    ff = w_gate.shape[2]
    micros, rows, width = tokens.shape
    rows_n, rows_f = half * near, half * micros * far
    vmem = pl.BlockSpec(memory_space=pltpu.VMEM)
    block = split_columns(ff)
    n_shape = (micros, half, near, width)
    f_shape = (half, micros * far, width)
    bf16 = jnp.bfloat16
    dma = pltpu.SemaphoreType.DMA
    return pl.pallas_call(
        functools.partial(layer, near, far, slots, experts),
        out_shape=jax.ShapeDtypeStruct((micros, rows, width), bf16),
        in_specs=[vmem] * 5 + [pl.BlockSpec(memory_space=pl.ANY)] * 3,
        out_specs=vmem,
        scratch_shapes=[
            pltpu.VMEM(w_gate.shape, bf16),
            pltpu.VMEM(w_up.shape, bf16),
            pltpu.VMEM(w_down.shape, bf16),
            pltpu.VMEM((micros, rows, width), bf16),
            pltpu.VMEM((micros, rows_n, rows), bf16),
            pltpu.VMEM((micros, rows_f, rows), bf16),
            pltpu.VMEM((slots * (ff // block), rows_n + rows_f, block), bf16),
            pltpu.VMEM((micros, rows, width), bf16),
            pltpu.VMEM(n_shape, bf16),
            pltpu.VMEM(f_shape, bf16),
            pltpu.VMEM(n_shape, bf16),
            pltpu.VMEM(f_shape, bf16),
            pltpu.VMEM(n_shape, bf16),
            pltpu.VMEM(f_shape, bf16),
            pltpu.VMEM(n_shape, bf16),
            pltpu.VMEM(f_shape, bf16),
            dma((3, slots)),
            dma((micros, half)),
            dma((micros, half)),
            dma((half,)),
            dma((half,)),
            dma((micros, half)),
            dma((micros, half)),
            dma((half,)),
            dma((half,)),
            dma((micros,)),
            dma((micros,)),
        ],
        compiler_params=pltpu.CompilerParams(
            collective_id=call, has_side_effects=True, vmem_limit_bytes=62 << 20
        ),
    )(tokens, gain, ids, scores, table, w_gate, w_up, w_down)


def body(tokens, norm_gain, expert_ids, route_scores, placement, w_gate, w_up, w_down):
    devices = lax.axis_size("expert")
    half = devices // 2
    slots = w_gate.shape[0]
    micros, _, rows, width = tokens.shape
    top = expert_ids.shape[3]
    experts = placement.shape[0] * 3 // 8
    most = (rows * top + experts - 1) // experts
    slot_cap = (most + 1) // 2
    arrays = (
        tokens[:, 0],
        norm_gain[None, :],
        jnp.swapaxes(expert_ids[:, 0], 1, 2),
        jnp.swapaxes(route_scores[:, 0], 1, 2),
        w_gate,
        w_up,
        w_down,
    )

    def plain():
        near = round_up(slots * slot_cap, 16)
        far = round_up(slots * slot_cap, 8)
        table = plain_table(placement, devices, slot_cap, near, far, micros)
        return routed(0, near, far, experts, table, *arrays)

    if devices != 8 or slots < 2:
        return plain()[:, None]
    near = round_up(rows * top // half, 16)
    far = near * 3 // 8
    rows_all = half * (near + far * micros)
    vmem = pl.BlockSpec(memory_space=pltpu.VMEM)
    table, fits = pl.pallas_call(
        functools.partial(plan, near, far, micros, experts, most),
        out_shape=(
            jax.ShapeDtypeStruct((rows_all, 128), jnp.int32),
            jax.ShapeDtypeStruct((8, 128), jnp.int32),
        ),
        in_specs=[vmem],
        out_specs=(vmem, vmem),
    )(placement.reshape(devices, slots))
    result = lax.cond(
        fits[0, 0] > 0, lambda: routed(1, near, far, experts, table, *arrays), plain
    )
    return result[:, None]


def solution(mesh):
    in_specs = (
        P(None, "section", "expert", None),
        P(),
        P(None, "section", "expert", None),
        P(None, "section", "expert", None),
        P(),
        P("expert", None, None),
        P("expert", None, None),
        P("expert", None, None),
    )
    out_specs = P(None, "section", "expert", None)
    return jax.shard_map(body, mesh=mesh, in_specs=in_specs, out_specs=out_specs, check_vma=False)
```

```python
import functools
import math

import jax
import jax.numpy as jnp
from jax import lax
from jax.experimental import pallas as pl
from jax.experimental.pallas import tpu as pltpu
from jax.sharding import PartitionSpec as P

EPSILON = 1e-06
STRIDE = 1024
MARK = 1 << 20
MESH = pl.DeviceIdType.MESH
COLUMNS = 256
PIECES = 4


def round_up(value, to):
    return (value + to - 1) // to * to


def split_columns(width):
    return COLUMNS if width % COLUMNS == 0 else width


def layer(
    near, far, slots, experts,
    tokens, gain, ids, scores, table, w_gate, w_up, w_down,
    out,
    gate_buf, up_buf, down_buf, normed, hits_near, hits_far, hidden, mixed, partial,
    send_n, send_f, recv_n, recv_f, done_n, done_f, back_n, back_f,
    weight_sem, to_n, from_n, to_f, from_f, ret_to_n, ret_from_n, ret_to_f, ret_from_f, relay_to, relay_from,
):
    section = lax.axis_index("section")
    sections = lax.axis_size("section")
    me = lax.axis_index("expert")
    peers = lax.axis_size("expert")
    half = peers // 2
    mine = me % half
    side = me // half
    micros, rows, width = tokens.shape
    top = ids.shape[1]
    rows_n, rows_f = half * near, half * far * micros

    for kind, (src, dst) in enumerate(((w_gate, gate_buf), (w_up, up_buf), (w_down, down_buf))):
        for slot in range(slots):
            if kind != 1:
                pltpu.make_async_copy(src.at[slot], dst.at[slot], weight_sem.at[kind, slot]).start()
            if kind == 0:
                pltpu.make_async_copy(w_up.at[slot], up_buf.at[slot], weight_sem.at[1, slot]).start()

    barrier = pltpu.get_barrier_semaphore()

    def greet(step, carry):
        pl.semaphore_signal(
            barrier, inc=1, device_id=(section, (me + step) % peers), device_id_type=MESH
        )
        return carry

    lax.fori_loop(1, peers, greet, 0)

    @pl.when(section > 0)
    def _():
        pl.semaphore_signal(barrier, inc=1, device_id=(section - 1, me), device_id_type=MESH)

    @pl.when(section < sections - 1)
    def _():
        pl.semaphore_signal(barrier, inc=1, device_id=(section + 1, me), device_id_type=MESH)

    kinds = round_up(experts, 16)
    kind = lax.broadcasted_iota(jnp.int32, (kinds, rows), 0)
    earlier = (
        lax.broadcasted_iota(jnp.int32, (rows, rows), 0)
        < lax.broadcasted_iota(jnp.int32, (rows, rows), 1)
    ).astype(jnp.bfloat16)
    code_near, code_far = table[:rows_n, 0:1], table[rows_n:, 0:1]
    mixing = []
    for micro in range(micros):
        values = tokens[micro].astype(jnp.float32)
        scale = lax.rsqrt(jnp.mean(values * values, axis=-1, keepdims=True) + EPSILON)
        normed[micro] = (values * scale * gain[...]).astype(jnp.bfloat16)
        ones = [(ids[micro, k : k + 1, :] == kind).astype(jnp.float32) for k in range(top)]
        both = functools.reduce(jnp.add, ones)
        before = jnp.dot(both.astype(jnp.bfloat16), earlier, preferred_element_type=jnp.float32)
        chosen = [scores[micro, k : k + 1, :] for k in range(top)]
        whole = functools.reduce(jnp.add, chosen)
        take_n = take_f = mix_n = mix_f = 0.0
        for k in range(top):
            rank = jnp.sum(before * ones[k], axis=0, keepdims=True).astype(jnp.int32)
            code = ids[micro, k : k + 1, :] * STRIDE + rank
            prob = chosen[k] / whole
            in_n = (code == code_near).astype(jnp.float32)
            in_f = (code + micro * MARK == code_far).astype(jnp.float32)
            take_n = take_n + in_n
            take_f = take_f + in_f
            mix_n = mix_n + in_n * prob
            mix_f = mix_f + in_f * prob
        hits_near[micro] = take_n.astype(jnp.bfloat16)
        hits_far[micro] = take_f.astype(jnp.bfloat16)
        mixing.append((mix_n, mix_f))

    def gather(hits, source):
        return jnp.dot(hits, source, preferred_element_type=jnp.float32)

    greeted = (
        peers - 1 + (section > 0).astype(jnp.int32) + (section < sections - 1).astype(jnp.int32)
    )
    pl.semaphore_wait(barrier, greeted)

    def far_copy(step, src, dst, sent, arrived):
        there = (mine + step) % half
        return pltpu.make_async_remote_copy(
            src_ref=src.at[there],
            dst_ref=dst.at[mine],
            send_sem=sent.at[step],
            recv_sem=arrived.at[step],
            device_id=(section, (1 - side) * half + there),
            device_id_type=MESH,
        )

    def near_copy(micro, step, src, dst, sent, arrived):
        there = (mine + step) % half
        return pltpu.make_async_remote_copy(
            src_ref=src.at[micro, there],
            dst_ref=dst.at[micro, mine],
            send_sem=sent.at[micro, step],
            recv_sem=arrived.at[micro, step],
            device_id=(section, side * half + there),
            device_id_type=MESH,
        )

    def each(first, act):
        def step_body(step, carry):
            act(step)
            return carry

        lax.fori_loop(first, half, step_body, 0)

    for micro in range(micros):
        send_n[micro] = (
            gather(hits_near[micro], normed[micro]).astype(jnp.bfloat16).reshape(send_n.shape[1:])
        )
        each(1, lambda step: near_copy(micro, step, send_n, recv_n, to_n, from_n).start())
        recv_n[micro, mine] = send_n[micro, mine]
        if micro == 0:
            send_f[...] = (
                sum(gather(hits_far[micro], normed[micro]) for micro in range(micros))
                .astype(jnp.bfloat16)
                .reshape(send_f.shape)
            )
            each(0, lambda step: far_copy(step, send_f, recv_f, to_f, from_f).start())

    def load(kind, slot):
        src, dst = ((w_gate, gate_buf), (w_up, up_buf), (w_down, down_buf))[kind]
        return pltpu.make_async_copy(src.at[slot], dst.at[slot], weight_sem.at[kind, slot])

    def loaded(kinds):
        def loaded_body(slot, carry):
            for kind in kinds:
                load(kind, slot).wait()
            return carry

        lax.fori_loop(0, slots, loaded_body, 0)

    def experts_of(count, inputs, owner, store, fresh=False, sent=None):
        ff = gate_buf.shape[2]
        block = split_columns(ff)
        per = ff // block

        def up_body(step, carry):
            slot = step // per
            if fresh:

                @pl.when(step % per == 0)
                def _():
                    load(0, slot).wait()
                    load(1, slot).wait()

            cols = pl.ds(pl.multiple_of((step % per) * block, block), block)
            x = inputs()
            gate = jnp.dot(x, gate_buf[slot, :, cols], preferred_element_type=jnp.float32)
            up = jnp.dot(x, up_buf[slot, :, cols], preferred_element_type=jnp.float32)
            unit = gate / (1.0 + jnp.exp(-gate)) * up
            unit = jnp.where(owner == slot, unit, 0.0)
            hidden[step, :count] = unit.astype(jnp.bfloat16)
            return carry

        lax.fori_loop(0, slots * per, up_body, 0)
        if fresh:
            loaded((2,))
        wide = split_columns(width)
        group = width // wide // PIECES

        def down_body(step, carry):
            cols = pl.ds(pl.multiple_of(step * wide, wide), wide)
            total = jnp.zeros((count, wide), jnp.float32)
            for slot in range(slots):
                for part in range(per):
                    total = total + jnp.dot(
                        hidden[slot * per + part, :count],
                        down_buf[slot, part * block : (part + 1) * block, cols],
                        preferred_element_type=jnp.float32,
                    )
            store(cols, total.astype(jnp.bfloat16))
            if sent is not None:

                @pl.when(step % group == group - 1)
                def _():
                    sent(step // group)

            return carry

        lax.fori_loop(0, width // wide, down_body, 0)

    for micro in range(micros):
        each(1, lambda step: near_copy(micro, step, send_n, recv_n, to_n, from_n).wait_recv())

        def store_near(cols, value):
            done_n[micro, :, :, cols] = value.reshape(half, near, value.shape[1])

        experts_of(
            rows_n,
            lambda: recv_n[micro].reshape(rows_n, width),
            table[:rows_n, 1:2],
            store_near,
            fresh=micro == 0,
        )
        each(1, lambda step: near_copy(micro, step, done_n, back_n, ret_to_n, ret_from_n).start())
        back_n[micro, mine] = done_n[micro, mine]

    piece = width // PIECES

    def far_return(step, part):
        there = (mine + step) % half
        cols = pl.ds(pl.multiple_of(part * piece, piece), piece)
        return pltpu.make_async_remote_copy(
            src_ref=done_f.at[there, :, cols],
            dst_ref=back_f.at[mine, :, cols],
            send_sem=ret_to_f.at[part, step],
            recv_sem=ret_from_f.at[part, step],
            device_id=(section, (1 - side) * half + there),
            device_id_type=MESH,
        )

    def store_far(cols, value):
        done_f[:, :, cols] = value.reshape(half, far * micros, value.shape[1])

    each(0, lambda step: far_copy(step, send_f, recv_f, to_f, from_f).wait_recv())
    experts_of(
        rows_f,
        lambda: recv_f[...].reshape(rows_f, width),
        table[rows_n:, 1:2],
        store_far,
        sent=lambda part: each(0, lambda step: far_return(step, part).start()),
    )

    def weighed(mix, values):
        high = mix.astype(jnp.bfloat16)
        low = (mix - high.astype(jnp.float32)).astype(jnp.bfloat16)
        rule = (((0,), (0,)), ((), ()))
        return lax.dot_general(
            high, values, rule, preferred_element_type=jnp.float32
        ) + lax.dot_general(low, values, rule, preferred_element_type=jnp.float32)

    def relay(micro, by, part):
        cols = pl.ds(part * piece, piece)
        return pltpu.make_async_remote_copy(
            src_ref=mixed.at[micro, :, cols],
            dst_ref=out.at[micro, :, cols],
            send_sem=relay_to.at[micro, part],
            recv_sem=relay_from.at[micro, part],
            device_id=(section + by, me),
            device_id_type=MESH,
        )

    sends = ((0, 1, section < sections - 1, section > 0), (1, -1, section > 0, section < sections - 1))
    for micro, by, gives, gets in sends:
        each(1, lambda step: near_copy(micro, step, done_n, back_n, ret_to_n, ret_from_n).wait_recv())
        partial[micro] = tokens[micro].astype(jnp.float32) + weighed(
            mixing[micro][0], back_n[micro].reshape(rows_n, width)
        )

        @pl.when(jnp.logical_not(gets))
        def _():
            out[micro] = jnp.zeros(out.shape[1:], out.dtype)

    for part in range(PIECES):
        cols = pl.ds(part * piece, piece)
        each(0, lambda step: far_return(step, part).wait_recv())
        for micro, by, gives, gets in sends:
            total = partial[micro, :, cols] + weighed(
                mixing[micro][1], back_f[:, :, cols].reshape(rows_f, piece)
            )
            mixed[micro, :, cols] = total.astype(jnp.bfloat16)

            @pl.when(gives)
            def _():
                relay(micro, by, part).start()

    each(0, lambda step: far_copy(step, send_f, recv_f, to_f, from_f).wait_send())
    for part in range(PIECES):
        each(0, lambda step: far_return(step, part).wait_send())
    for micro in range(micros):
        each(1, lambda step: near_copy(micro, step, send_n, recv_n, to_n, from_n).wait_send())
        each(1, lambda step: near_copy(micro, step, done_n, back_n, ret_to_n, ret_from_n).wait_send())
    for micro, by, gives, gets in sends:
        for part in range(PIECES):

            @pl.when(gives)
            def _():
                relay(micro, by, part).wait_send()

            @pl.when(gets)
            def _():
                relay(micro, by, part).wait_recv()


def plain_table(placement, devices, slot_cap, near, far, micros):
    half = devices // 2
    side = lax.axis_index("expert") // half
    slots = placement.shape[0]
    per = slots // devices
    slot_range = jnp.arange(slots, dtype=jnp.int32)
    same = placement[:, None] == placement[None, :]
    copies = jnp.sum(same, axis=1, dtype=jnp.int32)
    replica = jnp.sum(same & (slot_range[None, :] < slot_range[:, None]), axis=1, dtype=jnp.int32)
    index = jnp.arange(slot_cap, dtype=jnp.int32)
    code = placement[:, None] * STRIDE + index[None, :] * copies[:, None] + replica[:, None]
    code = code.reshape(devices, per * slot_cap)
    owner = jnp.broadcast_to(jnp.arange(per, dtype=jnp.int32)[:, None], (per, slot_cap)).reshape(-1)
    fill_n, fill_f = near - per * slot_cap, far - per * slot_cap
    code_n = jnp.pad(code, ((0, 0), (0, fill_n)), constant_values=-1)
    code_f = jnp.pad(code, ((0, 0), (0, fill_f)), constant_values=-1)
    code_n = lax.dynamic_slice_in_dim(code_n, side * half, half, 0).reshape(-1)
    code_f = lax.dynamic_slice_in_dim(code_f, (1 - side) * half, half, 0)[:, None, :]
    marks = jnp.arange(micros, dtype=jnp.int32)[None, :, None] * MARK
    code_f = jnp.where(code_f >= 0, code_f + marks, -1).reshape(-1)
    slot_n = jnp.tile(jnp.pad(owner, (0, fill_n)), half)
    slot_f = jnp.tile(jnp.pad(owner, (0, fill_f)), half * micros)
    columns = jnp.stack(
        [jnp.concatenate([code_n, code_f]), jnp.concatenate([slot_n, slot_f])], axis=1
    )
    return jnp.pad(columns, ((0, 0), (0, 126)))


def plan(devices, near, far, micros, experts, most, held, table, fits):
    per = held.shape[1] // devices
    half = devices // 2
    me = lax.axis_index("expert")
    side = me // half
    f32 = jnp.float32
    shape = (devices, 128)
    lane = lax.broadcasted_iota(jnp.int32, shape, 1)
    device = lax.broadcasted_iota(jnp.int32, shape, 0)
    from_half = lane // 64
    attempt = lane % 64
    strides = [a for a in range(1, experts) if math.gcd(a, experts) == 1][: max(1, 64 // experts)]
    turn = attempt // experts
    stride = jnp.full(shape, strides[0], jnp.int32)
    for i, a in enumerate(strides):
        stride = jnp.where(turn == i, a, stride)
    weight = jnp.where(device // half == from_half, far, near)
    limit = near * far
    spot = lax.broadcasted_iota(jnp.int32, (devices, held.shape[1]), 1)
    first_spot = lax.broadcasted_iota(jnp.int32, (devices, held.shape[1]), 0) * per
    owned = [
        jnp.sum(jnp.where(spot == first_spot + j, held[...], 0).astype(f32), axis=1, keepdims=True)
        .astype(jnp.int32)
        for j in range(per)
    ]
    order, holds = [], []
    now = attempt % experts
    for _ in range(experts):
        order.append(now)
        holds.append(functools.reduce(jnp.logical_or, [o == now for o in owned]))
        now = now + stride
        now = jnp.where(now >= experts, now - experts, now)
    load = jnp.zeros(shape, jnp.int32)
    given = [jnp.zeros(shape, jnp.int32)] * experts
    chunks = [most - most // 2, most // 2]
    for _ in range(2):
        for step in range(experts):
            load = load - given[step]
            share = jnp.zeros(shape, jnp.int32)
            for chunk in chunks:
                key = jnp.where(holds[step], (load + chunk) * weight * devices + device, 1 << 30)
                best = jnp.min(key, axis=0, keepdims=True)
                more = jnp.where(key == best, chunk, 0)
                load = load + more
                share = share + more
            given[step] = share
    worst = jnp.max(load * weight, axis=0, keepdims=True)
    lane_row = lax.broadcasted_iota(jnp.int32, (1, 128), 1)
    rating = worst * 128 + lane_row
    half_row = lane_row // 64
    ratings = [
        jnp.min(jnp.where(half_row == h, rating, 1 << 30), axis=1, keepdims=True) for h in range(2)
    ]
    fits[0] = (jnp.max(jnp.maximum(ratings[0], ratings[1])) < (limit + 1) * 128).astype(jnp.int32)

    def columns(from_side, length, width, period, to_device):
        rating_there = jnp.where(from_side == 0, ratings[0], ratings[1])
        picked = (rating == rating_there) & (half_row == from_side)
        amount = jnp.zeros(shape, f32)
        kinds = jnp.zeros((1, 128), f32)
        for step in range(experts):
            mine = jnp.sum(jnp.where(picked, given[step], 0).astype(f32), axis=1, keepdims=True)
            kind = jnp.sum(
                jnp.where(picked, order[step][:1], 0).astype(f32), axis=1, keepdims=True
            )
            amount = amount + jnp.where(lane == step, mine, 0.0)
            kinds = kinds + jnp.where(lane_row == step, kind, 0.0)
        first = jnp.dot(
            (
                lax.broadcasted_iota(jnp.int32, (devices, devices), 1)
                < lax.broadcasted_iota(jnp.int32, (devices, devices), 0)
            ).astype(f32),
            amount,
            preferred_element_type=f32,
        )
        ahead = jnp.dot(
            amount,
            (
                lax.broadcasted_iota(jnp.int32, (128, 128), 0)
                < lax.broadcasted_iota(jnp.int32, (128, 128), 1)
            ).astype(f32),
            preferred_element_type=f32,
        )
        local = jnp.zeros(shape, f32)
        for j in reversed(range(per)):
            local = jnp.where(owned[j].astype(f32) == kinds, float(j), local)
        row = lax.broadcasted_iota(jnp.int32, (length, 1), 0)
        place = (row % period).astype(f32)
        target = (
            lax.broadcasted_iota(jnp.int32, (length, devices), 1) == to_device(row // width)
        ).astype(f32)

        def spread(values):
            return jnp.dot(target, values, preferred_element_type=f32)

        start = spread(ahead)
        inside = ((place >= start) & (place < start + spread(amount))).astype(f32)
        numbers = kinds * STRIDE + place - start + spread(first)
        code = jnp.sum(inside * (numbers + 1.0), axis=1, keepdims=True).astype(jnp.int32) - 1
        slot = jnp.sum(inside * spread(local), axis=1, keepdims=True).astype(jnp.int32)
        return code, slot, row

    rows_n, rows_f = half * near, half * far * micros
    code_n, _, _ = columns(side, rows_n, near, near, lambda block: side * half + block)
    code_f, _, row_f = columns(
        side, rows_f, far * micros, far, lambda block: (1 - side) * half + block
    )
    code_f = jnp.where(code_f >= 0, code_f + row_f % (far * micros) // far * MARK, -1)
    _, slot_n, _ = columns(side, rows_n, near, near, lambda block: me + 0 * block)
    _, slot_f, _ = columns(1 - side, rows_f, far * micros, far, lambda block: me + 0 * block)
    column = lax.broadcasted_iota(jnp.int32, (rows_n, 128), 1)
    table[:rows_n] = jnp.where(column == 0, code_n, slot_n)
    column = lax.broadcasted_iota(jnp.int32, (rows_f, 128), 1)
    table[rows_n:] = jnp.where(column == 0, code_f, slot_f)


def routed(call, near, far, experts, table, tokens, gain, ids, scores, w_gate, w_up, w_down):
    devices = lax.axis_size("expert")
    half = devices // 2
    slots = w_gate.shape[0]
    ff = w_gate.shape[2]
    micros, rows, width = tokens.shape
    rows_n, rows_f = half * near, half * micros * far
    vmem = pl.BlockSpec(memory_space=pltpu.VMEM)
    block = split_columns(ff)
    n_shape = (micros, half, near, width)
    f_shape = (half, micros * far, width)
    bf16 = jnp.bfloat16
    dma = pltpu.SemaphoreType.DMA
    return pl.pallas_call(
        functools.partial(layer, near, far, slots, experts),
        out_shape=jax.ShapeDtypeStruct((micros, rows, width), bf16),
        in_specs=[vmem] * 5 + [pl.BlockSpec(memory_space=pl.ANY)] * 3,
        out_specs=vmem,
        scratch_shapes=[
            pltpu.VMEM(w_gate.shape, bf16),
            pltpu.VMEM(w_up.shape, bf16),
            pltpu.VMEM(w_down.shape, bf16),
            pltpu.VMEM((micros, rows, width), bf16),
            pltpu.VMEM((micros, rows_n, rows), bf16),
            pltpu.VMEM((micros, rows_f, rows), bf16),
            pltpu.VMEM((slots * (ff // block), max(rows_n, rows_f), block), bf16),
            pltpu.VMEM((micros, rows, width), bf16),
            pltpu.VMEM((micros, rows, width), jnp.float32),
            pltpu.VMEM(n_shape, bf16),
            pltpu.VMEM(f_shape, bf16),
            pltpu.VMEM(n_shape, bf16),
            pltpu.VMEM(f_shape, bf16),
            pltpu.VMEM(n_shape, bf16),
            pltpu.VMEM(f_shape, bf16),
            pltpu.VMEM(n_shape, bf16),
            pltpu.VMEM(f_shape, bf16),
            dma((3, slots)),
            dma((micros, half)),
            dma((micros, half)),
            dma((half,)),
            dma((half,)),
            dma((micros, half)),
            dma((micros, half)),
            dma((PIECES, half)),
            dma((PIECES, half)),
            dma((micros, PIECES)),
            dma((micros, PIECES)),
        ],
        compiler_params=pltpu.CompilerParams(
            collective_id=call, has_side_effects=True, vmem_limit_bytes=62 << 20
        ),
    )(tokens, gain, ids, scores, table, w_gate, w_up, w_down)


def body(tokens, norm_gain, expert_ids, route_scores, placement, w_gate, w_up, w_down):
    devices = lax.axis_size("expert")
    half = devices // 2
    slots = w_gate.shape[0]
    micros, _, rows, width = tokens.shape
    top = expert_ids.shape[3]
    experts = placement.shape[0] * 3 // 8
    most = (rows * top + experts - 1) // experts
    slot_cap = (most + 1) // 2
    arrays = (
        tokens[:, 0],
        norm_gain[None, :],
        jnp.swapaxes(expert_ids[:, 0], 1, 2),
        jnp.swapaxes(route_scores[:, 0], 1, 2),
        w_gate,
        w_up,
        w_down,
    )

    def plain():
        near = round_up(slots * slot_cap, 16)
        far = round_up(slots * slot_cap, 8)
        table = plain_table(placement, devices, slot_cap, near, far, micros)
        return routed(0, near, far, experts, table, *arrays)

    if devices != 8 or slots < 2:
        return plain()[:, None]
    near = round_up(rows * top // half, 16)
    far = near * 3 // 8
    rows_all = half * (near + far * micros)
    vmem = pl.BlockSpec(memory_space=pltpu.VMEM)
    table, fits = pl.pallas_call(
        functools.partial(plan, devices, near, far, micros, experts, most),
        out_shape=(
            jax.ShapeDtypeStruct((rows_all, 128), jnp.int32),
            jax.ShapeDtypeStruct((1,), jnp.int32),
        ),
        in_specs=[vmem],
        out_specs=(vmem, pl.BlockSpec(memory_space=pltpu.SMEM)),
    )(placement[None, :])
    result = lax.cond(
        fits[0] > 0, lambda: routed(1, near, far, experts, table, *arrays), plain
    )
    return result[:, None]


def solution(mesh):
    in_specs = (
        P(None, "section", "expert", None),
        P(),
        P(None, "section", "expert", None),
        P(None, "section", "expert", None),
        P(),
        P("expert", None, None),
        P("expert", None, None),
        P("expert", None, None),
    )
    out_specs = P(None, "section", "expert", None)
    return jax.shard_map(body, mesh=mesh, in_specs=in_specs, out_specs=out_specs, check_vma=False)
```

```python
import functools
import math

import jax
import jax.numpy as jnp
from jax import lax
from jax.experimental import pallas as pl
from jax.experimental.pallas import tpu as pltpu
from jax.sharding import PartitionSpec as P

EPSILON = 1e-06
STRIDE = 1024
MARK = 1 << 20
MESH = pl.DeviceIdType.MESH
PIECES = 4


def round_up(value, to):
    return (value + to - 1) // to * to


def layer(
    near, far, slots, experts,
    tokens, gain, ids, scores, table, w_gate, w_up, w_down,
    out,
    gate_buf, up_buf, down_buf, normed, hits_near, hits_far, hidden, mixed, partial, far_rows,
    send_n, send_f, recv_n, recv_f, done_n, done_f, back_n, back_f,
    weight_sem, to_n, from_n, to_f, from_f, ret_to_n, ret_from_n, ret_to_f, ret_from_f, relay_to, relay_from,
):
    section = lax.axis_index("section")
    sections = lax.axis_size("section")
    me = lax.axis_index("expert")
    peers = lax.axis_size("expert")
    half = peers // 2
    mine = me % half
    side = me // half
    micros, rows, width = tokens.shape
    top = ids.shape[1]
    rows_n, rows_f = half * near, half * far * micros

    for kind, (src, dst) in enumerate(((w_gate, gate_buf), (w_up, up_buf), (w_down, down_buf))):
        for slot in range(slots):
            if kind != 1:
                pltpu.make_async_copy(src.at[slot], dst.at[slot], weight_sem.at[kind, slot]).start()
            if kind == 0:
                pltpu.make_async_copy(w_up.at[slot], up_buf.at[slot], weight_sem.at[1, slot]).start()

    barrier = pltpu.get_barrier_semaphore()

    def greet(step, carry):
        pl.semaphore_signal(
            barrier, inc=1, device_id=(section, (me + step) % peers), device_id_type=MESH
        )
        return carry

    lax.fori_loop(1, peers, greet, 0)

    @pl.when(section > 0)
    def _():
        pl.semaphore_signal(barrier, inc=1, device_id=(section - 1, me), device_id_type=MESH)

    @pl.when(section < sections - 1)
    def _():
        pl.semaphore_signal(barrier, inc=1, device_id=(section + 1, me), device_id_type=MESH)

    kinds = round_up(experts, 16)
    kind = lax.broadcasted_iota(jnp.int32, (kinds, rows), 0)
    earlier = (
        lax.broadcasted_iota(jnp.int32, (rows, rows), 0)
        < lax.broadcasted_iota(jnp.int32, (rows, rows), 1)
    ).astype(jnp.bfloat16)
    code_near, code_far = table[:rows_n, 0:1], table[rows_n:, 0:1]
    mixing = []
    for micro in range(micros):
        values = tokens[micro].astype(jnp.float32)
        scale = lax.rsqrt(jnp.mean(values * values, axis=-1, keepdims=True) + EPSILON)
        normed[micro] = (values * scale * gain[...]).astype(jnp.bfloat16)
        ones = [(ids[micro, k : k + 1, :] == kind).astype(jnp.float32) for k in range(top)]
        both = functools.reduce(jnp.add, ones)
        before = jnp.dot(both.astype(jnp.bfloat16), earlier, preferred_element_type=jnp.float32)
        chosen = [scores[micro, k : k + 1, :] for k in range(top)]
        whole = functools.reduce(jnp.add, chosen)
        take_n = take_f = mix_n = mix_f = 0.0
        for k in range(top):
            rank = jnp.sum(before * ones[k], axis=0, keepdims=True).astype(jnp.int32)
            code = ids[micro, k : k + 1, :] * STRIDE + rank
            prob = chosen[k] / whole
            in_n = (code == code_near).astype(jnp.float32)
            in_f = (code + micro * MARK == code_far).astype(jnp.float32)
            take_n = take_n + in_n
            take_f = take_f + in_f
            mix_n = mix_n + in_n * prob
            mix_f = mix_f + in_f * prob
        hits_near[micro] = take_n.astype(jnp.bfloat16)
        hits_far[micro] = take_f.astype(jnp.bfloat16)
        mixing.append((mix_n, mix_f))

    def gather(hits, source):
        return jnp.dot(hits, source, preferred_element_type=jnp.float32)

    greeted = (
        peers - 1 + (section > 0).astype(jnp.int32) + (section < sections - 1).astype(jnp.int32)
    )
    pl.semaphore_wait(barrier, greeted)

    def far_copy(step, src, dst, sent, arrived):
        there = (mine + step) % half
        return pltpu.make_async_remote_copy(
            src_ref=src.at[there],
            dst_ref=dst.at[mine],
            send_sem=sent.at[step],
            recv_sem=arrived.at[step],
            device_id=(section, (1 - side) * half + there),
            device_id_type=MESH,
        )

    def near_copy(micro, step, src, dst, sent, arrived):
        there = (mine + step) % half
        return pltpu.make_async_remote_copy(
            src_ref=src.at[micro, there],
            dst_ref=dst.at[micro, mine],
            send_sem=sent.at[micro, step],
            recv_sem=arrived.at[micro, step],
            device_id=(section, side * half + there),
            device_id_type=MESH,
        )

    def each(first, act):
        def step_body(step, carry):
            act(step)
            return carry

        lax.fori_loop(first, half, step_body, 0)

    for micro in range(micros):
        send_n[micro] = (
            gather(hits_near[micro], normed[micro]).astype(jnp.bfloat16).reshape(send_n.shape[1:])
        )
        each(1, lambda step: near_copy(micro, step, send_n, recv_n, to_n, from_n).start())
        recv_n[micro, mine] = send_n[micro, mine]
    send_f[...] = (
        sum(gather(hits_far[micro], normed[micro]) for micro in range(micros))
        .astype(jnp.bfloat16)
        .reshape(send_f.shape)
    )
    each(0, lambda step: far_copy(step, send_f, recv_f, to_f, from_f).start())

    def load(kind, slot):
        src, dst = ((w_gate, gate_buf), (w_up, up_buf), (w_down, down_buf))[kind]
        return pltpu.make_async_copy(src.at[slot], dst.at[slot], weight_sem.at[kind, slot])

    def loaded(kinds):
        def loaded_body(slot, carry):
            for kind in kinds:
                load(kind, slot).wait()
            return carry

        lax.fori_loop(0, slots, loaded_body, 0)

    def experts_of(count, inputs, owner, store, fresh=False, sent=None):
        ff = gate_buf.shape[2]
        block = hidden.shape[2]
        per = ff // block

        def up_body(step, carry):
            slot = step // per
            if fresh:

                @pl.when(step % per == 0)
                def _():
                    load(0, slot).wait()
                    load(1, slot).wait()

            cols = pl.ds(pl.multiple_of((step % per) * block, block), block)
            x = inputs()
            gate = jnp.dot(x, gate_buf[slot, :, cols], preferred_element_type=jnp.float32)
            up = jnp.dot(x, up_buf[slot, :, cols], preferred_element_type=jnp.float32)
            unit = gate / (1.0 + jnp.exp(-gate)) * up
            unit = jnp.where(owner == slot, unit, 0.0)
            hidden[step, :count] = unit.astype(jnp.bfloat16)
            return carry

        lax.fori_loop(0, slots * per, up_body, 0)
        if fresh:
            loaded((2,))
        wide = width // PIECES

        def down_body(step, carry):
            cols = pl.ds(pl.multiple_of(step * wide, wide), wide)
            total = jnp.zeros((count, wide), jnp.float32)
            for slot in range(slots):
                for part in range(per):
                    total = total + jnp.dot(
                        hidden[slot * per + part, :count],
                        down_buf[slot, part * block : (part + 1) * block, cols],
                        preferred_element_type=jnp.float32,
                    )
            store(cols, total.astype(jnp.bfloat16))
            if sent is not None:
                sent(step)

            return carry

        lax.fori_loop(0, width // wide, down_body, 0)

    for micro in range(micros):
        each(1, lambda step: near_copy(micro, step, send_n, recv_n, to_n, from_n).wait_recv())

    def store_near(cols, value):
        done_n[:, :, :, cols] = value.reshape(micros, half, near, value.shape[1])

    experts_of(
        rows_n * micros,
        lambda: recv_n[...].reshape(rows_n * micros, width),
        jnp.concatenate([table[:rows_n, 1:2]] * micros, axis=0),
        store_near,
        fresh=True,
    )
    for micro in range(micros):
        each(1, lambda step: near_copy(micro, step, done_n, back_n, ret_to_n, ret_from_n).start())
        back_n[micro, mine] = done_n[micro, mine]

    piece = width // PIECES

    def far_return(step, part):
        there = (mine + step) % half
        cols = pl.ds(pl.multiple_of(part * piece, piece), piece)
        return pltpu.make_async_remote_copy(
            src_ref=done_f.at[there, :, cols],
            dst_ref=back_f.at[mine, :, cols],
            send_sem=ret_to_f.at[part, step],
            recv_sem=ret_from_f.at[part, step],
            device_id=(section, (1 - side) * half + there),
            device_id_type=MESH,
        )

    def store_far(cols, value):
        done_f[:, :, cols] = value.reshape(half, far * micros, value.shape[1])

    each(0, lambda step: far_copy(step, send_f, recv_f, to_f, from_f).wait_recv())
    far_rows[...] = recv_f[...].reshape(rows_f, width)
    experts_of(
        rows_f,
        lambda: far_rows[...],
        table[rows_n:, 1:2],
        store_far,
        sent=lambda part: each(0, lambda step: far_return(step, part).start()),
    )

    def weighed(mix, values):
        high = mix.astype(jnp.bfloat16)
        low = (mix - high.astype(jnp.float32)).astype(jnp.bfloat16)
        rule = (((0,), (0,)), ((), ()))
        return lax.dot_general(
            high, values, rule, preferred_element_type=jnp.float32
        ) + lax.dot_general(low, values, rule, preferred_element_type=jnp.float32)

    def relay(micro, by, part):
        cols = pl.ds(part * piece, piece)
        return pltpu.make_async_remote_copy(
            src_ref=mixed.at[micro, :, cols],
            dst_ref=out.at[micro, :, cols],
            send_sem=relay_to.at[micro, part],
            recv_sem=relay_from.at[micro, part],
            device_id=(section + by, me),
            device_id_type=MESH,
        )

    sends = ((0, 1, section < sections - 1, section > 0), (1, -1, section > 0, section < sections - 1))
    for micro, by, gives, gets in sends:
        each(1, lambda step: near_copy(micro, step, done_n, back_n, ret_to_n, ret_from_n).wait_recv())
        partial[micro] = tokens[micro].astype(jnp.float32) + weighed(
            mixing[micro][0], back_n[micro].reshape(rows_n, width)
        )

        @pl.when(jnp.logical_not(gets))
        def _():
            out[micro] = jnp.zeros(out.shape[1:], out.dtype)

    for part in range(PIECES):
        cols = pl.ds(part * piece, piece)
        each(0, lambda step: far_return(step, part).wait_recv())
        for micro, by, gives, gets in sends:
            total = partial[micro, :, cols] + weighed(
                mixing[micro][1], back_f[:, :, cols].reshape(rows_f, piece)
            )
            mixed[micro, :, cols] = total.astype(jnp.bfloat16)

            @pl.when(gives)
            def _():
                relay(micro, by, part).start()

    each(0, lambda step: far_copy(step, send_f, recv_f, to_f, from_f).wait_send())
    for part in range(PIECES):
        each(0, lambda step: far_return(step, part).wait_send())
    for micro in range(micros):
        each(1, lambda step: near_copy(micro, step, send_n, recv_n, to_n, from_n).wait_send())
        each(1, lambda step: near_copy(micro, step, done_n, back_n, ret_to_n, ret_from_n).wait_send())
    for micro, by, gives, gets in sends:
        for part in range(PIECES):

            @pl.when(gives)
            def _():
                relay(micro, by, part).wait_send()

            @pl.when(gets)
            def _():
                relay(micro, by, part).wait_recv()


def plain_table(placement, devices, slot_cap, near, far, micros):
    half = devices // 2
    side = lax.axis_index("expert") // half
    slots = placement.shape[0]
    per = slots // devices
    slot_range = jnp.arange(slots, dtype=jnp.int32)
    same = placement[:, None] == placement[None, :]
    copies = jnp.sum(same, axis=1, dtype=jnp.int32)
    replica = jnp.sum(same & (slot_range[None, :] < slot_range[:, None]), axis=1, dtype=jnp.int32)
    index = jnp.arange(slot_cap, dtype=jnp.int32)
    code = placement[:, None] * STRIDE + index[None, :] * copies[:, None] + replica[:, None]
    code = code.reshape(devices, per * slot_cap)
    owner = jnp.broadcast_to(jnp.arange(per, dtype=jnp.int32)[:, None], (per, slot_cap)).reshape(-1)
    fill_n, fill_f = near - per * slot_cap, far - per * slot_cap
    code_n = jnp.pad(code, ((0, 0), (0, fill_n)), constant_values=-1)
    code_f = jnp.pad(code, ((0, 0), (0, fill_f)), constant_values=-1)
    code_n = lax.dynamic_slice_in_dim(code_n, side * half, half, 0).reshape(-1)
    code_f = lax.dynamic_slice_in_dim(code_f, (1 - side) * half, half, 0)[:, None, :]
    marks = jnp.arange(micros, dtype=jnp.int32)[None, :, None] * MARK
    code_f = jnp.where(code_f >= 0, code_f + marks, -1).reshape(-1)
    slot_n = jnp.tile(jnp.pad(owner, (0, fill_n)), half)
    slot_f = jnp.tile(jnp.pad(owner, (0, fill_f)), half * micros)
    columns = jnp.stack(
        [jnp.concatenate([code_n, code_f]), jnp.concatenate([slot_n, slot_f])], axis=1
    )
    return jnp.pad(columns, ((0, 0), (0, 126)))


def plan(devices, near, far, micros, experts, most, held, table, fits):
    per = held.shape[1] // devices
    half = devices // 2
    me = lax.axis_index("expert")
    side = me // half
    f32 = jnp.float32
    shape = (devices, 128)
    lane = lax.broadcasted_iota(jnp.int32, shape, 1)
    device = lax.broadcasted_iota(jnp.int32, shape, 0)
    from_half = lane // 64
    attempt = lane % 64
    strides = [a for a in range(1, experts) if math.gcd(a, experts) == 1][: max(1, 64 // experts)]
    turn = attempt // experts
    stride = jnp.full(shape, strides[0], jnp.int32)
    for i, a in enumerate(strides):
        stride = jnp.where(turn == i, a, stride)
    weight = jnp.where(device // half == from_half, far, near)
    limit = near * far
    spot = lax.broadcasted_iota(jnp.int32, (devices, held.shape[1]), 1)
    first_spot = lax.broadcasted_iota(jnp.int32, (devices, held.shape[1]), 0) * per
    owned = [
        jnp.sum(jnp.where(spot == first_spot + j, held[...], 0).astype(f32), axis=1, keepdims=True)
        .astype(jnp.int32)
        for j in range(per)
    ]
    order, holds = [], []
    now = attempt % experts
    for _ in range(experts):
        order.append(now)
        holds.append(functools.reduce(jnp.logical_or, [o == now for o in owned]))
        now = now + stride
        now = jnp.where(now >= experts, now - experts, now)
    load = jnp.zeros(shape, jnp.int32)
    given = [jnp.zeros(shape, jnp.int32)] * experts
    chunks = [most - most // 2, most // 2]
    for _ in range(2):
        for step in range(experts):
            load = load - given[step]
            share = jnp.zeros(shape, jnp.int32)
            for chunk in chunks:
                key = jnp.where(holds[step], (load + chunk) * weight * devices + device, 1 << 30)
                best = jnp.min(key, axis=0, keepdims=True)
                more = jnp.where(key == best, chunk, 0)
                load = load + more
                share = share + more
            given[step] = share
    worst = jnp.max(load * weight, axis=0, keepdims=True)
    lane_row = lax.broadcasted_iota(jnp.int32, (1, 128), 1)
    rating = worst * 128 + lane_row
    half_row = lane_row // 64
    ratings = [
        jnp.min(jnp.where(half_row == h, rating, 1 << 30), axis=1, keepdims=True) for h in range(2)
    ]
    fits[0] = (jnp.max(jnp.maximum(ratings[0], ratings[1])) < (limit + 1) * 128).astype(jnp.int32)

    def columns(from_side, length, width, period, to_device):
        rating_there = jnp.where(from_side == 0, ratings[0], ratings[1])
        picked = (rating == rating_there) & (half_row == from_side)
        amount = jnp.zeros(shape, f32)
        kinds = jnp.zeros((1, 128), f32)
        for step in range(experts):
            mine = jnp.sum(jnp.where(picked, given[step], 0).astype(f32), axis=1, keepdims=True)
            kind = jnp.sum(
                jnp.where(picked, order[step][:1], 0).astype(f32), axis=1, keepdims=True
            )
            amount = amount + jnp.where(lane == step, mine, 0.0)
            kinds = kinds + jnp.where(lane_row == step, kind, 0.0)
        first = jnp.dot(
            (
                lax.broadcasted_iota(jnp.int32, (devices, devices), 1)
                < lax.broadcasted_iota(jnp.int32, (devices, devices), 0)
            ).astype(f32),
            amount,
            preferred_element_type=f32,
        )
        ahead = jnp.dot(
            amount,
            (
                lax.broadcasted_iota(jnp.int32, (128, 128), 0)
                < lax.broadcasted_iota(jnp.int32, (128, 128), 1)
            ).astype(f32),
            preferred_element_type=f32,
        )
        local = jnp.zeros(shape, f32)
        for j in reversed(range(per)):
            local = jnp.where(owned[j].astype(f32) == kinds, float(j), local)
        row = lax.broadcasted_iota(jnp.int32, (length, 1), 0)
        place = (row % period).astype(f32)
        target = (
            lax.broadcasted_iota(jnp.int32, (length, devices), 1) == to_device(row // width)
        ).astype(f32)

        def spread(values):
            return jnp.dot(target, values, preferred_element_type=f32)

        start = spread(ahead)
        inside = ((place >= start) & (place < start + spread(amount))).astype(f32)
        numbers = kinds * STRIDE + place - start + spread(first)
        code = jnp.sum(inside * (numbers + 1.0), axis=1, keepdims=True).astype(jnp.int32) - 1
        slot = jnp.sum(inside * spread(local), axis=1, keepdims=True).astype(jnp.int32)
        return code, slot, row

    rows_n, rows_f = half * near, half * far * micros
    code_n, _, _ = columns(side, rows_n, near, near, lambda block: side * half + block)
    code_f, _, row_f = columns(
        side, rows_f, far * micros, far, lambda block: (1 - side) * half + block
    )
    code_f = jnp.where(code_f >= 0, code_f + row_f % (far * micros) // far * MARK, -1)
    _, slot_n, _ = columns(side, rows_n, near, near, lambda block: me + 0 * block)
    _, slot_f, _ = columns(1 - side, rows_f, far * micros, far, lambda block: me + 0 * block)
    column = lax.broadcasted_iota(jnp.int32, (rows_n, 128), 1)
    table[:rows_n] = jnp.where(column == 0, code_n, slot_n)
    column = lax.broadcasted_iota(jnp.int32, (rows_f, 128), 1)
    table[rows_n:] = jnp.where(column == 0, code_f, slot_f)


def routed(call, near, far, experts, table, tokens, gain, ids, scores, w_gate, w_up, w_down):
    devices = lax.axis_size("expert")
    half = devices // 2
    slots = w_gate.shape[0]
    ff = w_gate.shape[2]
    micros, rows, width = tokens.shape
    rows_n, rows_f = half * near, half * micros * far
    vmem = pl.BlockSpec(memory_space=pltpu.VMEM)
    block = ff
    n_shape = (micros, half, near, width)
    f_shape = (half, micros * far, width)
    bf16 = jnp.bfloat16
    dma = pltpu.SemaphoreType.DMA
    return pl.pallas_call(
        functools.partial(layer, near, far, slots, experts),
        out_shape=jax.ShapeDtypeStruct((micros, rows, width), bf16),
        in_specs=[vmem] * 5 + [pl.BlockSpec(memory_space=pl.ANY)] * 3,
        out_specs=vmem,
        scratch_shapes=[
            pltpu.VMEM(w_gate.shape, bf16),
            pltpu.VMEM(w_up.shape, bf16),
            pltpu.VMEM(w_down.shape, bf16),
            pltpu.VMEM((micros, rows, width), bf16),
            pltpu.VMEM((micros, rows_n, rows), bf16),
            pltpu.VMEM((micros, rows_f, rows), bf16),
            pltpu.VMEM((slots * (ff // block), max(rows_n * micros, rows_f), block), bf16),
            pltpu.VMEM((micros, rows, width), bf16),
            pltpu.VMEM((micros, rows, width), jnp.float32),
            pltpu.VMEM((rows_f, width), bf16),
            pltpu.VMEM(n_shape, bf16),
            pltpu.VMEM(f_shape, bf16),
            pltpu.VMEM(n_shape, bf16),
            pltpu.VMEM(f_shape, bf16),
            pltpu.VMEM(n_shape, bf16),
            pltpu.VMEM(f_shape, bf16),
            pltpu.VMEM(n_shape, bf16),
            pltpu.VMEM(f_shape, bf16),
            dma((3, slots)),
            dma((micros, half)),
            dma((micros, half)),
            dma((half,)),
            dma((half,)),
            dma((micros, half)),
            dma((micros, half)),
            dma((PIECES, half)),
            dma((PIECES, half)),
            dma((micros, PIECES)),
            dma((micros, PIECES)),
        ],
        compiler_params=pltpu.CompilerParams(
            collective_id=call, has_side_effects=True, vmem_limit_bytes=62 << 20
        ),
    )(tokens, gain, ids, scores, table, w_gate, w_up, w_down)


def body(tokens, norm_gain, expert_ids, route_scores, placement, w_gate, w_up, w_down):
    devices = lax.axis_size("expert")
    half = devices // 2
    slots = w_gate.shape[0]
    micros, _, rows, width = tokens.shape
    top = expert_ids.shape[3]
    experts = placement.shape[0] * 3 // 8
    most = (rows * top + experts - 1) // experts
    slot_cap = (most + 1) // 2
    arrays = (
        tokens[:, 0],
        norm_gain[None, :],
        jnp.swapaxes(expert_ids[:, 0], 1, 2),
        jnp.swapaxes(route_scores[:, 0], 1, 2),
        w_gate,
        w_up,
        w_down,
    )

    def plain():
        near = round_up(slots * slot_cap, 16)
        far = round_up(slots * slot_cap, 8)
        table = plain_table(placement, devices, slot_cap, near, far, micros)
        return routed(0, near, far, experts, table, *arrays)

    if devices != 8 or slots < 2:
        return plain()[:, None]
    near = round_up(rows * top // half, 16)
    far = near * 3 // 8
    rows_all = half * (near + far * micros)
    vmem = pl.BlockSpec(memory_space=pltpu.VMEM)
    table, fits = pl.pallas_call(
        functools.partial(plan, devices, near, far, micros, experts, most),
        out_shape=(
            jax.ShapeDtypeStruct((rows_all, 128), jnp.int32),
            jax.ShapeDtypeStruct((1,), jnp.int32),
        ),
        in_specs=[vmem],
        out_specs=(vmem, pl.BlockSpec(memory_space=pltpu.SMEM)),
    )(placement[None, :])
    result = lax.cond(
        fits[0] > 0, lambda: routed(1, near, far, experts, table, *arrays), plain
    )
    return result[:, None]


def solution(mesh):
    in_specs = (
        P(None, "section", "expert", None),
        P(),
        P(None, "section", "expert", None),
        P(None, "section", "expert", None),
        P(),
        P("expert", None, None),
        P("expert", None, None),
        P("expert", None, None),
    )
    out_specs = P(None, "section", "expert", None)
    return jax.shard_map(body, mesh=mesh, in_specs=in_specs, out_specs=out_specs, check_vma=False)
```

```python
import functools
import math

import jax
import jax.numpy as jnp
from jax import lax
from jax.experimental import pallas as pl
from jax.experimental.pallas import tpu as pltpu
from jax.sharding import PartitionSpec as P

EPSILON = 1e-06
STRIDE = 1024
MARK = 1 << 20
MESH = pl.DeviceIdType.MESH
PIECES = 4


def round_up(value, to):
    return (value + to - 1) // to * to


def layer(
    near, far, slots, experts,
    tokens, gain, ids, scores, table, w_gate, w_up, w_down,
    out,
    gate_buf, up_buf, down_buf, normed, hits_near, hits_far, hidden, mixed, partial, all_rows,
    send_n, send_f, recv_n, recv_f, done_n, done_f, back_n, back_f,
    weight_sem, to_n, from_n, to_f, from_f, ret_to_n, ret_from_n, ret_to_f, ret_from_f, relay_to, relay_from,
):
    section = lax.axis_index("section")
    sections = lax.axis_size("section")
    me = lax.axis_index("expert")
    peers = lax.axis_size("expert")
    half = peers // 2
    mine = me % half
    side = me // half
    micros, rows, width = tokens.shape
    top = ids.shape[1]
    rows_n, rows_f = half * near, half * far * micros

    for kind, (src, dst) in enumerate(((w_gate, gate_buf), (w_up, up_buf), (w_down, down_buf))):
        for slot in range(slots):
            if kind != 1:
                pltpu.make_async_copy(src.at[slot], dst.at[slot], weight_sem.at[kind, slot]).start()
            if kind == 0:
                pltpu.make_async_copy(w_up.at[slot], up_buf.at[slot], weight_sem.at[1, slot]).start()

    barrier = pltpu.get_barrier_semaphore()

    def greet(step, carry):
        pl.semaphore_signal(
            barrier, inc=1, device_id=(section, (me + step) % peers), device_id_type=MESH
        )
        return carry

    lax.fori_loop(1, peers, greet, 0)

    @pl.when(section > 0)
    def _():
        pl.semaphore_signal(barrier, inc=1, device_id=(section - 1, me), device_id_type=MESH)

    @pl.when(section < sections - 1)
    def _():
        pl.semaphore_signal(barrier, inc=1, device_id=(section + 1, me), device_id_type=MESH)

    kinds = round_up(experts, 16)
    kind = lax.broadcasted_iota(jnp.int32, (kinds, rows), 0)
    earlier = (
        lax.broadcasted_iota(jnp.int32, (rows, rows), 0)
        < lax.broadcasted_iota(jnp.int32, (rows, rows), 1)
    ).astype(jnp.bfloat16)
    code_near, code_far = table[:rows_n, 0:1], table[rows_n:, 0:1]
    mixing = []
    for micro in range(micros):
        values = tokens[micro].astype(jnp.float32)
        scale = lax.rsqrt(jnp.mean(values * values, axis=-1, keepdims=True) + EPSILON)
        normed[micro] = (values * scale * gain[...]).astype(jnp.bfloat16)
        ones = [(ids[micro, k : k + 1, :] == kind).astype(jnp.float32) for k in range(top)]
        both = functools.reduce(jnp.add, ones)
        before = jnp.dot(both.astype(jnp.bfloat16), earlier, preferred_element_type=jnp.float32)
        chosen = [scores[micro, k : k + 1, :] for k in range(top)]
        whole = functools.reduce(jnp.add, chosen)
        take_n = take_f = mix_n = mix_f = 0.0
        for k in range(top):
            rank = jnp.sum(before * ones[k], axis=0, keepdims=True).astype(jnp.int32)
            code = ids[micro, k : k + 1, :] * STRIDE + rank
            prob = chosen[k] / whole
            in_n = (code == code_near).astype(jnp.float32)
            in_f = (code + micro * MARK == code_far).astype(jnp.float32)
            take_n = take_n + in_n
            take_f = take_f + in_f
            mix_n = mix_n + in_n * prob
            mix_f = mix_f + in_f * prob
        hits_near[micro] = take_n.astype(jnp.bfloat16)
        hits_far[micro] = take_f.astype(jnp.bfloat16)
        mixing.append((mix_n, mix_f))

    def gather(hits, source):
        return jnp.dot(hits, source, preferred_element_type=jnp.float32)

    greeted = (
        peers - 1 + (section > 0).astype(jnp.int32) + (section < sections - 1).astype(jnp.int32)
    )
    pl.semaphore_wait(barrier, greeted)

    def far_copy(step, src, dst, sent, arrived):
        there = (mine + step) % half
        return pltpu.make_async_remote_copy(
            src_ref=src.at[there],
            dst_ref=dst.at[mine],
            send_sem=sent.at[step],
            recv_sem=arrived.at[step],
            device_id=(section, (1 - side) * half + there),
            device_id_type=MESH,
        )

    def near_copy(micro, step, src, dst, sent, arrived):
        there = (mine + step) % half
        return pltpu.make_async_remote_copy(
            src_ref=src.at[micro, there],
            dst_ref=dst.at[micro, mine],
            send_sem=sent.at[micro, step],
            recv_sem=arrived.at[micro, step],
            device_id=(section, side * half + there),
            device_id_type=MESH,
        )

    def each(first, act):
        def step_body(step, carry):
            act(step)
            return carry

        lax.fori_loop(first, half, step_body, 0)

    for micro in range(micros):
        send_n[micro] = (
            gather(hits_near[micro], normed[micro]).astype(jnp.bfloat16).reshape(send_n.shape[1:])
        )
        each(1, lambda step: near_copy(micro, step, send_n, recv_n, to_n, from_n).start())
        recv_n[micro, mine] = send_n[micro, mine]
    send_f[...] = (
        sum(gather(hits_far[micro], normed[micro]) for micro in range(micros))
        .astype(jnp.bfloat16)
        .reshape(send_f.shape)
    )
    each(0, lambda step: far_copy(step, send_f, recv_f, to_f, from_f).start())

    def load(kind, slot):
        src, dst = ((w_gate, gate_buf), (w_up, up_buf), (w_down, down_buf))[kind]
        return pltpu.make_async_copy(src.at[slot], dst.at[slot], weight_sem.at[kind, slot])

    def loaded(kinds):
        def loaded_body(slot, carry):
            for kind in kinds:
                load(kind, slot).wait()
            return carry

        lax.fori_loop(0, slots, loaded_body, 0)

    def experts_of(count, inputs, owner, store, fresh=False, sent=None):
        ff = gate_buf.shape[2]
        block = hidden.shape[2]
        per = ff // block

        def up_body(step, carry):
            slot = step // per
            if fresh:

                @pl.when(step % per == 0)
                def _():
                    load(0, slot).wait()
                    load(1, slot).wait()

            cols = pl.ds(pl.multiple_of((step % per) * block, block), block)
            x = inputs()
            gate = jnp.dot(x, gate_buf[slot, :, cols], preferred_element_type=jnp.float32)
            up = jnp.dot(x, up_buf[slot, :, cols], preferred_element_type=jnp.float32)
            unit = gate / (1.0 + jnp.exp(-gate)) * up
            unit = jnp.where(owner == slot, unit, 0.0)
            hidden[step, :count] = unit.astype(jnp.bfloat16)
            return carry

        lax.fori_loop(0, slots * per, up_body, 0)
        if fresh:
            loaded((2,))
        wide = width // PIECES

        def down_body(step, carry):
            cols = pl.ds(pl.multiple_of(step * wide, wide), wide)
            total = jnp.zeros((count, wide), jnp.float32)
            for slot in range(slots):
                for part in range(per):
                    total = total + jnp.dot(
                        hidden[slot * per + part, :count],
                        down_buf[slot, part * block : (part + 1) * block, cols],
                        preferred_element_type=jnp.float32,
                    )
            store(cols, total.astype(jnp.bfloat16))
            if sent is not None:
                sent(step)

            return carry

        lax.fori_loop(0, width // wide, down_body, 0)

    for micro in range(micros):
        each(1, lambda step: near_copy(micro, step, send_n, recv_n, to_n, from_n).wait_recv())

    all_rows[rows_f:] = recv_n[...].reshape(rows_n * micros, width)

    piece = width // PIECES

    def far_return(step, part):
        there = (mine + step) % half
        cols = pl.ds(pl.multiple_of(part * piece, piece), piece)
        return pltpu.make_async_remote_copy(
            src_ref=done_f.at[there, :, cols],
            dst_ref=back_f.at[mine, :, cols],
            send_sem=ret_to_f.at[part, step],
            recv_sem=ret_from_f.at[part, step],
            device_id=(section, (1 - side) * half + there),
            device_id_type=MESH,
        )

    def store_all(cols, value):
        done_f[:, :, cols] = value[:rows_f].reshape(half, far * micros, value.shape[1])
        done_n[:, :, :, cols] = value[rows_f:].reshape(micros, half, near, value.shape[1])

    each(0, lambda step: far_copy(step, send_f, recv_f, to_f, from_f).wait_recv())
    all_rows[:rows_f] = recv_f[...].reshape(rows_f, width)
    experts_of(
        rows_f + rows_n * micros,
        lambda: all_rows[...],
        jnp.concatenate([table[rows_n:, 1:2]] + [table[:rows_n, 1:2]] * micros, axis=0),
        store_all,
        fresh=True,
        sent=lambda part: each(0, lambda step: far_return(step, part).start()),
    )
    for micro in range(micros):
        each(1, lambda step: near_copy(micro, step, done_n, back_n, ret_to_n, ret_from_n).start())
        back_n[micro, mine] = done_n[micro, mine]

    def weighed(mix, values):
        high = mix.astype(jnp.bfloat16)
        low = (mix - high.astype(jnp.float32)).astype(jnp.bfloat16)
        rule = (((0,), (0,)), ((), ()))
        return lax.dot_general(
            high, values, rule, preferred_element_type=jnp.float32
        ) + lax.dot_general(low, values, rule, preferred_element_type=jnp.float32)

    def relay(micro, by, part):
        cols = pl.ds(part * piece, piece)
        return pltpu.make_async_remote_copy(
            src_ref=mixed.at[micro, :, cols],
            dst_ref=out.at[micro, :, cols],
            send_sem=relay_to.at[micro, part],
            recv_sem=relay_from.at[micro, part],
            device_id=(section + by, me),
            device_id_type=MESH,
        )

    sends = ((0, 1, section < sections - 1, section > 0), (1, -1, section > 0, section < sections - 1))
    for micro, by, gives, gets in sends:
        each(1, lambda step: near_copy(micro, step, done_n, back_n, ret_to_n, ret_from_n).wait_recv())
        partial[micro] = tokens[micro].astype(jnp.float32) + weighed(
            mixing[micro][0], back_n[micro].reshape(rows_n, width)
        )

        @pl.when(jnp.logical_not(gets))
        def _():
            out[micro] = jnp.zeros(out.shape[1:], out.dtype)

    for part in range(PIECES):
        cols = pl.ds(part * piece, piece)
        each(0, lambda step: far_return(step, part).wait_recv())
        for micro, by, gives, gets in sends:
            total = partial[micro, :, cols] + weighed(
                mixing[micro][1], back_f[:, :, cols].reshape(rows_f, piece)
            )
            mixed[micro, :, cols] = total.astype(jnp.bfloat16)

            @pl.when(gives)
            def _():
                relay(micro, by, part).start()

    each(0, lambda step: far_copy(step, send_f, recv_f, to_f, from_f).wait_send())
    for part in range(PIECES):
        each(0, lambda step: far_return(step, part).wait_send())
    for micro in range(micros):
        each(1, lambda step: near_copy(micro, step, send_n, recv_n, to_n, from_n).wait_send())
        each(1, lambda step: near_copy(micro, step, done_n, back_n, ret_to_n, ret_from_n).wait_send())
    for micro, by, gives, gets in sends:
        for part in range(PIECES):

            @pl.when(gives)
            def _():
                relay(micro, by, part).wait_send()

            @pl.when(gets)
            def _():
                relay(micro, by, part).wait_recv()


def plain_table(placement, devices, slot_cap, near, far, micros):
    half = devices // 2
    side = lax.axis_index("expert") // half
    slots = placement.shape[0]
    per = slots // devices
    slot_range = jnp.arange(slots, dtype=jnp.int32)
    same = placement[:, None] == placement[None, :]
    copies = jnp.sum(same, axis=1, dtype=jnp.int32)
    replica = jnp.sum(same & (slot_range[None, :] < slot_range[:, None]), axis=1, dtype=jnp.int32)
    index = jnp.arange(slot_cap, dtype=jnp.int32)
    code = placement[:, None] * STRIDE + index[None, :] * copies[:, None] + replica[:, None]
    code = code.reshape(devices, per * slot_cap)
    owner = jnp.broadcast_to(jnp.arange(per, dtype=jnp.int32)[:, None], (per, slot_cap)).reshape(-1)
    fill_n, fill_f = near - per * slot_cap, far - per * slot_cap
    code_n = jnp.pad(code, ((0, 0), (0, fill_n)), constant_values=-1)
    code_f = jnp.pad(code, ((0, 0), (0, fill_f)), constant_values=-1)
    code_n = lax.dynamic_slice_in_dim(code_n, side * half, half, 0).reshape(-1)
    code_f = lax.dynamic_slice_in_dim(code_f, (1 - side) * half, half, 0)[:, None, :]
    marks = jnp.arange(micros, dtype=jnp.int32)[None, :, None] * MARK
    code_f = jnp.where(code_f >= 0, code_f + marks, -1).reshape(-1)
    slot_n = jnp.tile(jnp.pad(owner, (0, fill_n)), half)
    slot_f = jnp.tile(jnp.pad(owner, (0, fill_f)), half * micros)
    columns = jnp.stack(
        [jnp.concatenate([code_n, code_f]), jnp.concatenate([slot_n, slot_f])], axis=1
    )
    return jnp.pad(columns, ((0, 0), (0, 126)))


def plan(devices, near, far, micros, experts, most, held, table, fits):
    per = held.shape[1] // devices
    half = devices // 2
    me = lax.axis_index("expert")
    side = me // half
    f32 = jnp.float32
    shape = (devices, 128)
    lane = lax.broadcasted_iota(jnp.int32, shape, 1)
    device = lax.broadcasted_iota(jnp.int32, shape, 0)
    from_half = lane // 64
    attempt = lane % 64
    strides = [a for a in range(1, experts) if math.gcd(a, experts) == 1][: max(1, 64 // experts)]
    turn = attempt // experts
    stride = jnp.full(shape, strides[0], jnp.int32)
    for i, a in enumerate(strides):
        stride = jnp.where(turn == i, a, stride)
    weight = jnp.where(device // half == from_half, far, near)
    limit = near * far
    spot = lax.broadcasted_iota(jnp.int32, (devices, held.shape[1]), 1)
    first_spot = lax.broadcasted_iota(jnp.int32, (devices, held.shape[1]), 0) * per
    owned = [
        jnp.sum(jnp.where(spot == first_spot + j, held[...], 0).astype(f32), axis=1, keepdims=True)
        .astype(jnp.int32)
        for j in range(per)
    ]
    order, holds = [], []
    now = attempt % experts
    for _ in range(experts):
        order.append(now)
        holds.append(functools.reduce(jnp.logical_or, [o == now for o in owned]))
        now = now + stride
        now = jnp.where(now >= experts, now - experts, now)
    load = jnp.zeros(shape, jnp.int32)
    given = [jnp.zeros(shape, jnp.int32)] * experts
    chunks = [most - most // 2, most // 2]
    for _ in range(2):
        for step in range(experts):
            load = load - given[step]
            share = jnp.zeros(shape, jnp.int32)
            for chunk in chunks:
                key = jnp.where(holds[step], (load + chunk) * weight * devices + device, 1 << 30)
                best = jnp.min(key, axis=0, keepdims=True)
                more = jnp.where(key == best, chunk, 0)
                load = load + more
                share = share + more
            given[step] = share
    worst = jnp.max(load * weight, axis=0, keepdims=True)
    lane_row = lax.broadcasted_iota(jnp.int32, (1, 128), 1)
    rating = worst * 128 + lane_row
    half_row = lane_row // 64
    ratings = [
        jnp.min(jnp.where(half_row == h, rating, 1 << 30), axis=1, keepdims=True) for h in range(2)
    ]
    fits[0] = (jnp.max(jnp.maximum(ratings[0], ratings[1])) < (limit + 1) * 128).astype(jnp.int32)

    def columns(from_side, length, width, period, to_device):
        rating_there = jnp.where(from_side == 0, ratings[0], ratings[1])
        picked = (rating == rating_there) & (half_row == from_side)
        amount = jnp.zeros(shape, f32)
        kinds = jnp.zeros((1, 128), f32)
        for step in range(experts):
            mine = jnp.sum(jnp.where(picked, given[step], 0).astype(f32), axis=1, keepdims=True)
            kind = jnp.sum(
                jnp.where(picked, order[step][:1], 0).astype(f32), axis=1, keepdims=True
            )
            amount = amount + jnp.where(lane == step, mine, 0.0)
            kinds = kinds + jnp.where(lane_row == step, kind, 0.0)
        first = jnp.dot(
            (
                lax.broadcasted_iota(jnp.int32, (devices, devices), 1)
                < lax.broadcasted_iota(jnp.int32, (devices, devices), 0)
            ).astype(f32),
            amount,
            preferred_element_type=f32,
        )
        ahead = jnp.dot(
            amount,
            (
                lax.broadcasted_iota(jnp.int32, (128, 128), 0)
                < lax.broadcasted_iota(jnp.int32, (128, 128), 1)
            ).astype(f32),
            preferred_element_type=f32,
        )
        local = jnp.zeros(shape, f32)
        for j in reversed(range(per)):
            local = jnp.where(owned[j].astype(f32) == kinds, float(j), local)
        row = lax.broadcasted_iota(jnp.int32, (length, 1), 0)
        place = (row % period).astype(f32)
        target = (
            lax.broadcasted_iota(jnp.int32, (length, devices), 1) == to_device(row // width)
        ).astype(f32)

        def spread(values):
            return jnp.dot(target, values, preferred_element_type=f32)

        start = spread(ahead)
        inside = ((place >= start) & (place < start + spread(amount))).astype(f32)
        numbers = kinds * STRIDE + place - start + spread(first)
        code = jnp.sum(inside * (numbers + 1.0), axis=1, keepdims=True).astype(jnp.int32) - 1
        slot = jnp.sum(inside * spread(local), axis=1, keepdims=True).astype(jnp.int32)
        return code, slot, row

    rows_n, rows_f = half * near, half * far * micros
    code_n, _, _ = columns(side, rows_n, near, near, lambda block: side * half + block)
    code_f, _, row_f = columns(
        side, rows_f, far * micros, far, lambda block: (1 - side) * half + block
    )
    code_f = jnp.where(code_f >= 0, code_f + row_f % (far * micros) // far * MARK, -1)
    _, slot_n, _ = columns(side, rows_n, near, near, lambda block: me + 0 * block)
    _, slot_f, _ = columns(1 - side, rows_f, far * micros, far, lambda block: me + 0 * block)
    column = lax.broadcasted_iota(jnp.int32, (rows_n, 128), 1)
    table[:rows_n] = jnp.where(column == 0, code_n, slot_n)
    column = lax.broadcasted_iota(jnp.int32, (rows_f, 128), 1)
    table[rows_n:] = jnp.where(column == 0, code_f, slot_f)


def routed(call, near, far, experts, table, tokens, gain, ids, scores, w_gate, w_up, w_down):
    devices = lax.axis_size("expert")
    half = devices // 2
    slots = w_gate.shape[0]
    ff = w_gate.shape[2]
    micros, rows, width = tokens.shape
    rows_n, rows_f = half * near, half * micros * far
    vmem = pl.BlockSpec(memory_space=pltpu.VMEM)
    block = ff
    n_shape = (micros, half, near, width)
    f_shape = (half, micros * far, width)
    bf16 = jnp.bfloat16
    dma = pltpu.SemaphoreType.DMA
    return pl.pallas_call(
        functools.partial(layer, near, far, slots, experts),
        out_shape=jax.ShapeDtypeStruct((micros, rows, width), bf16),
        in_specs=[vmem] * 5 + [pl.BlockSpec(memory_space=pl.ANY)] * 3,
        out_specs=vmem,
        scratch_shapes=[
            pltpu.VMEM(w_gate.shape, bf16),
            pltpu.VMEM(w_up.shape, bf16),
            pltpu.VMEM(w_down.shape, bf16),
            pltpu.VMEM((micros, rows, width), bf16),
            pltpu.VMEM((micros, rows_n, rows), bf16),
            pltpu.VMEM((micros, rows_f, rows), bf16),
            pltpu.VMEM((slots * (ff // block), rows_n * micros + rows_f, block), bf16),
            pltpu.VMEM((micros, rows, width), bf16),
            pltpu.VMEM((micros, rows, width), jnp.float32),
            pltpu.VMEM((rows_f + rows_n * micros, width), bf16),
            pltpu.VMEM(n_shape, bf16),
            pltpu.VMEM(f_shape, bf16),
            pltpu.VMEM(n_shape, bf16),
            pltpu.VMEM(f_shape, bf16),
            pltpu.VMEM(n_shape, bf16),
            pltpu.VMEM(f_shape, bf16),
            pltpu.VMEM(n_shape, bf16),
            pltpu.VMEM(f_shape, bf16),
            dma((3, slots)),
            dma((micros, half)),
            dma((micros, half)),
            dma((half,)),
            dma((half,)),
            dma((micros, half)),
            dma((micros, half)),
            dma((PIECES, half)),
            dma((PIECES, half)),
            dma((micros, PIECES)),
            dma((micros, PIECES)),
        ],
        compiler_params=pltpu.CompilerParams(
            collective_id=call, has_side_effects=True, vmem_limit_bytes=62 << 20
        ),
    )(tokens, gain, ids, scores, table, w_gate, w_up, w_down)


def body(tokens, norm_gain, expert_ids, route_scores, placement, w_gate, w_up, w_down):
    devices = lax.axis_size("expert")
    half = devices // 2
    slots = w_gate.shape[0]
    micros, _, rows, width = tokens.shape
    top = expert_ids.shape[3]
    experts = placement.shape[0] * 3 // 8
    most = (rows * top + experts - 1) // experts
    slot_cap = (most + 1) // 2
    arrays = (
        tokens[:, 0],
        norm_gain[None, :],
        jnp.swapaxes(expert_ids[:, 0], 1, 2),
        jnp.swapaxes(route_scores[:, 0], 1, 2),
        w_gate,
        w_up,
        w_down,
    )

    def plain():
        near = round_up(slots * slot_cap, 16)
        far = round_up(slots * slot_cap, 8)
        table = plain_table(placement, devices, slot_cap, near, far, micros)
        return routed(0, near, far, experts, table, *arrays)

    if devices != 8 or slots < 2:
        return plain()[:, None]
    near = round_up(rows * top // half, 16)
    far = near * 3 // 8
    rows_all = half * (near + far * micros)
    vmem = pl.BlockSpec(memory_space=pltpu.VMEM)
    table, fits = pl.pallas_call(
        functools.partial(plan, devices, near, far, micros, experts, most),
        out_shape=(
            jax.ShapeDtypeStruct((rows_all, 128), jnp.int32),
            jax.ShapeDtypeStruct((1,), jnp.int32),
        ),
        in_specs=[vmem],
        out_specs=(vmem, pl.BlockSpec(memory_space=pltpu.SMEM)),
    )(placement[None, :])
    result = lax.cond(
        fits[0] > 0, lambda: routed(1, near, far, experts, table, *arrays), plain
    )
    return result[:, None]


def solution(mesh):
    in_specs = (
        P(None, "section", "expert", None),
        P(),
        P(None, "section", "expert", None),
        P(None, "section", "expert", None),
        P(),
        P("expert", None, None),
        P("expert", None, None),
        P("expert", None, None),
    )
    out_specs = P(None, "section", "expert", None)
    return jax.shard_map(body, mesh=mesh, in_specs=in_specs, out_specs=out_specs, check_vma=False)
```
